128 devices in a mesh: tx: 8 (over x, core), ty: 16 (over z, y).
Axes of the slice: x: 4, y: 4, z: 4, core: 2. Of those that a mesh axis runs over, the one named last changes fastest.
Arguments:
- cot_field: float32 [8, 2048, 8192], P(None, 'tx', 'ty'), may hold values from -6 to 6
- conductance: float32 [8, 2048, 8192], P(None, 'tx', 'ty'), may hold values from 0.04 to 0.16
- diagonal: float32 [8, 2048, 8192], P(None, 'tx', 'ty'), may hold values from 1 to 2
- source_adjoint: bfloat16 [262144, 128], P(('tx', 'ty')), may hold values from -6 to 6
- spreading: bfloat16 [16, 128, 128], replicated, may hold values from -0.5 to 0.5
- heat_deriv: float32 [262144, 128], P(('tx', 'ty')), may hold values from 0.25 to 1.75
- block_tile: int32 [262144, 1], P(('tx', 'ty')), may hold values from 0 to 127; in each aligned block of 2048 rows (0 to 2047, 2048 to 4095, ...) at most 32 rows name the same one
- block_patch: int32 [262144], P(('tx', 'ty')), may hold values from 0 to 8191
- block_kind: int32 [262144], P(('tx', 'ty')), may hold values from 0 to 15
Outputs:
- temp_adjoint: float32 [8, 2048, 8192], P(None, 'tx', 'ty')
- source_grad: float32 [262144, 128], P(('tx', 'ty'))
The draws below stay inside these ranges and needn't reach their ends.
Inputs may be any that keep to these rules, and one draw needn't show every extreme that they name: `block_tile`: among the blocks of one device, no tile is named by more than 32 blocks, a bound that some block reaches.
All inputs are finite; a program needn't handle non-finite values.
Results may differ from the reference program's by a relative error of at most 0.0018.
The reference program's roundings to bfloat16 on the way (of `heat_patch`) count: a program that leaves them out, or rounds other values in their place, can miss the bound.
Values may be sent and summed in bfloat16 or wider, within the bound.
A program may use at most 128 MiB of HBM per device.

```python
import math
import jax
import jax.numpy as jnp
import numpy as np
from jax import lax

NZ = 8
CX = 256
CY = 512
BLOCK_DEV = 2048
KINDS = 16
SWEEPS = 2
NX = 2048
NY = 8192
BLOCKS = 262144
CAP = 32
PATCHES = 8192
N_TY = 16
DEVICES = 128


def with_ends(array, key, low, largest):
    longest = array.shape.index(max(array.shape))
    spots = []
    for shift in (0, 1):
        where = [jax.random.randint(jax.random.fold_in(key, axis), (), 0, length) for axis, length in enumerate(array.shape)]
        where[longest] = (where[longest] + shift) % array.shape[longest]
        spots.append(tuple(where))
    return array.at[spots[0]].set(low).at[spots[1]].set(largest)


def steps_of(own_key, shape, cuts, low, high):
    def one(axis_at, shards_of):
        steps = jax.random.uniform(jax.random.fold_in(jax.random.fold_in(own_key, 6), axis_at), (shards_of,), jnp.float32, low / len(cuts), high / len(cuts))
        return jnp.repeat(jnp.exp(steps), shape[axis_at] // shards_of).reshape((-1,) + (1,) * (len(shape) - axis_at - 1))

    factor_of = one(*cuts[0])
    for cut in cuts[1:]:
        factor_of = factor_of * one(*cut)
    return factor_of


def assign_block(stream_key, own, number, rows, count, top, most, skew):
    order = jax.random.permutation(stream_key, count)
    heavy_load, ordinary = shares(count, rows * top, most, skew, True), shares(count, rows * top, most, skew, False)
    places = jnp.arange(count)

    def named(lengths, offset_by):
        used = int((lengths > 0).sum())
        fixed = max(1, used // 4)
        moved = fixed + (places - fixed + offset_by * (used - fixed)) % max(1, count - fixed)
        return jnp.zeros((count,), jnp.int32).at[order[jnp.where(places < fixed, places, moved)]].set(jnp.asarray(lengths, jnp.int32))

    lengths = jnp.where(number % 4 == 0, named(heavy_load, number // 4), named(ordinary, number - number // 4 - 1))
    mixed = jax.random.permutation(jax.random.fold_in(own, 3), count)
    giver, taker = mixed[0:count // 2 * 2:2], mixed[1:count // 2 * 2:2]
    slack = jnp.minimum(lengths[giver] - 1, most - lengths[taker]) // 2
    slack = jnp.where((giver == order[0]) | (taker == order[0]) | (lengths[taker] == 0), 0, jnp.maximum(slack, 0))
    moved = jax.random.randint(jax.random.fold_in(own, 4), (count // 2,), 0, 1 << 20) % (slack + 1)
    lengths = lengths.at[giver].add(-moved).at[taker].add(moved)
    labels = jnp.searchsorted(jnp.cumsum(lengths), jnp.arange(rows * top), side="right").astype(jnp.int32)
    grid = labels.reshape(top, rows).T
    grid = grid[jax.random.permutation(jax.random.fold_in(own, 1), rows)]
    offset_by = jax.random.randint(jax.random.fold_in(own, 2), (rows, 1), 0, top)
    return jnp.take_along_axis(grid, (jnp.arange(top)[None, :] + offset_by) % top, axis=1)


def shares(number_of, total, most, skew, full):
    loads = [(1 << 20) // math.isqrt(standing ** skew) + 1 for standing in range(1, number_of + 1)]
    largest = most if full else min(most, max(-(-total // number_of), total * loads[0] // sum(loads)))
    least = 1 if total - largest >= number_of - 1 else 0
    given, rest = [largest] + [least] * (number_of - 1), total - largest - least * (number_of - 1)
    while rest > 0:
        candidates = [i for i in range(1, number_of) if given[i] < largest] or [i for i in range(1, number_of) if given[i] < most]
        mass, left = sum([loads[i] for i in candidates]), rest
        for i in candidates:
            addition = min(most - given[i], max(1, left * loads[i] // mass), rest)
            given[i] = given[i] + addition
            rest = rest - addition
    return np.array(given)


def noise(own_key, shape, deviation, bound, split=(), held_as=jnp.bfloat16):
    factor_of = steps_of(own_key, shape, split, -0.22, 0.18) if split else 1.0
    result = jax.random.normal(own_key, shape, jnp.float32) * deviation * factor_of
    return jnp.minimum(jnp.maximum(result, -bound), bound).astype(held_as)


def setup_inputs(seed: int = 0) -> dict:
    streams_of = jax.random.split(jax.random.key(seed), 10)
    cot_field = noise(streams_of[0], (NZ, NX, NY), 1.0, 6.0, ((1, 8), (2, 16)), jnp.float32)
    conductance = jnp.clip(jnp.exp(math.log(0.16) - 1.3862944 * jax.random.uniform(streams_of[1], (NZ, NX, NY), jnp.float32) ** steps_of(streams_of[1], (NZ, NX, NY), ((1, 8), (2, 16)), -0.2, 0.2)), 0.04, 0.16)
    diagonal = jnp.clip(1.0 + 1.0 * jax.random.uniform(streams_of[2], (NZ, NX, NY), jnp.float32) ** steps_of(streams_of[2], (NZ, NX, NY), ((1, 8), (2, 16)), -0.2, 0.2), 1.0, 2.0)
    source_adjoint = noise(streams_of[3], (BLOCKS, 128), 1.0, 6.0, ((0, 128),))
    spreading = noise(streams_of[4], (KINDS, 128, 128), 128 ** -0.5, 0.5)
    heat_deriv = jnp.clip(1.0 + 0.15 * jax.random.normal(streams_of[5], (BLOCKS, 128), jnp.float32), 0.25, 1.75)
    block_tile_keys = jax.random.split(jax.random.fold_in(streams_of[6], 1), BLOCKS // BLOCK_DEV)
    block_tile_turns = jax.random.permutation(jax.random.fold_in(streams_of[6], 3), BLOCKS // BLOCK_DEV)
    block_tile = jax.vmap(lambda own, number: assign_block(jax.random.fold_in(streams_of[6], 2), own, number, BLOCK_DEV, DEVICES, 1, CAP, 2))(block_tile_keys, block_tile_turns).reshape((BLOCKS, 1))
    block_patch = with_ends(jax.random.randint(streams_of[7], (BLOCKS,), 0, PATCHES), jax.random.fold_in(streams_of[7], 1), 0, PATCHES - 1).astype(jnp.int32)
    block_kind = with_ends(jax.random.randint(streams_of[8], (BLOCKS,), 0, KINDS), jax.random.fold_in(streams_of[8], 1), 0, KINDS - 1).astype(jnp.int32)
    return dict(cot_field=cot_field, conductance=conductance, diagonal=diagonal, source_adjoint=source_adjoint, spreading=spreading, heat_deriv=heat_deriv, block_tile=block_tile, block_patch=block_patch, block_kind=block_kind)


def neighbours(padded):
    centre = padded[:, 1:-1, 1:-1]
    layered = jnp.pad(centre, ((1, 1), (0, 0), (0, 0)))
    total = padded[:, :-2, 1:-1] + padded[:, 2:, 1:-1]
    total = total + padded[:, 1:-1, :-2] + padded[:, 1:-1, 2:]
    return total + layered[:-2] + layered[2:]


def reference(cot_field, conductance, diagonal, source_adjoint, spreading, heat_deriv, block_tile, block_patch, block_kind):
    wide = spreading.astype(jnp.float32)

    def forward_one(pair):
        seeds, kinds = pair
        return jnp.einsum("bi,bij->bj", seeds.astype(jnp.float32), wide[kinds])

    cell_seed = lax.map(forward_one, (source_adjoint.reshape(DEVICES, BLOCK_DEV, 128), block_kind.reshape(DEVICES, BLOCK_DEV)))
    cell_seed = cell_seed.reshape(BLOCKS, 128)
    tiles = block_tile[:, 0]
    tile_row = tiles // N_TY
    tile_col = tiles % N_TY
    per_layer = CX * CY // 128
    layer = block_patch // per_layer
    row_local = (block_patch // (CY // 128)) % CX
    segment = block_patch % (CY // 128)
    row_global = (tile_row * CX + row_local).astype(jnp.int32)
    seg_global = (tile_col * (CY // 128) + segment).astype(jnp.int32)
    rhs = cot_field.reshape(NZ, NX, NY // 128, 128).at[layer, row_global, seg_global].add(cell_seed)
    rhs = rhs.reshape(NZ, NX, NY)
    inverse_diag = 1.0 / diagonal
    adjoint = rhs * inverse_diag
    for sweep_index in range(SWEEPS):
        padded = jnp.pad(conductance * adjoint, ((0, 0), (1, 1), (1, 1)))
        adjoint = (rhs + neighbours(padded)) * inverse_diag
    heat_patch = adjoint.reshape(NZ, NX, NY // 128, 128)[layer, row_global, seg_global].astype(jnp.bfloat16)

    def backward_one(pair):
        patches, kinds = pair
        return jnp.einsum("bj,bij->bi", patches.astype(jnp.float32), wide[kinds])

    pulled = lax.map(backward_one, (heat_patch.reshape(DEVICES, BLOCK_DEV, 128), block_kind.reshape(DEVICES, BLOCK_DEV)))
    source_grad = heat_deriv * pulled.reshape(BLOCKS, 128)
    return adjoint, source_grad
```

```python
import functools

import jax
import jax.numpy as jnp
from jax import lax
from jax.experimental import pallas as pl
from jax.experimental.pallas import tpu as pltpu
from jax.sharding import PartitionSpec as P

NX_DEV, NY_DEV = 8, 16
DEV = NX_DEV * NY_DEV
CAP = 32
SLOTS = DEV * CAP
KINDS = 16
NZ, CX, CY = 8, 256, 512
CH = CY // 128
PATCHES = NZ * CX * CH
ROWS = PATCHES + CAP
SEG = CX + 16
GROWS = CH * (NZ + 2) * SEG
OWNED = 2048
GROUP = 8
F32, BF16, I32 = jnp.float32, jnp.bfloat16, jnp.int32
MESH = pl.DeviceIdType.MESH
VMEM = pl.BlockSpec(memory_space=pltpu.VMEM)
SMEM = pl.BlockSpec(memory_space=pltpu.SMEM)
ANY = pl.BlockSpec(memory_space=pl.ANY)
NT = (((1,), (1,)), ((), ()))


def dot(a, b):
    return jnp.dot(a, b, preferred_element_type=F32)


def iota(shape, dim):
    return lax.broadcasted_iota(I32, shape, dim)


def route_kernel(
    tile_ref, patch_ref, kind_ref, src_ref,
    send_ref, meta_ref, slot_ref, kb_ref,
    srcf, sendf, slot_s, sem,
):
    sub, lane = iota((128, 128), 0), iota((128, 128), 1)
    before = (sub < lane).astype(F32).astype(BF16)
    ones = jnp.ones((128, 128), BF16)
    rank_row = iota((CAP, 128), 0)
    count = jnp.zeros((128, 128), F32)
    table = jnp.zeros((128, 128), F32)
    for j in range(OWNED // 128):
        tile = tile_ref[j : j + 1, :]
        patch = patch_ref[j : j + 1, :]
        kind = kind_ref[j : j + 1, :]
        place = (patch & (CH - 1)) * (NZ * CX) + (patch >> 2)
        hit = (sub == tile).astype(F32)
        hit16 = hit.astype(BF16)
        rank = jnp.sum(hit * (dot(hit16, before) + count), axis=0, keepdims=True).astype(I32)
        count = count + dot(hit16, ones)
        slot_ref[j : j + 1, :] = tile * CAP + rank
        at = (rank_row == rank).astype(F32)
        parts = jnp.concatenate(
            [
                at * (place >> 7).astype(F32),
                at * (place & 127).astype(F32),
                at * (kind + 1).astype(F32),
                jnp.zeros((128 - 3 * CAP, 128), F32),
            ],
            axis=0,
        ).astype(BF16)
        table = table + lax.dot_general(hit16, parts, NT, preferred_element_type=F32)
        kb_ref[pl.ds(j * 128, 128), :] = jnp.transpose(
            jnp.broadcast_to(kind.astype(F32), (128, 128))
        ).astype(BF16)
    copy = pltpu.make_async_copy(slot_ref, slot_s, sem)
    copy.start()
    counts = count.astype(I32)
    place = (table * 128.0 + pltpu.roll(table, 128 - CAP, 1)).astype(I32)
    kind1 = pltpu.roll(table, 128 - 2 * CAP, 1).astype(I32)
    place = jnp.where(lane < counts, place, PATCHES + lane)
    within = lane & (GROUP - 1)
    clash = jnp.zeros((128, 128), I32)
    for k in range(1, GROUP):
        same = (pltpu.roll(place, k, 1) == place) & (within >= k)
        clash = jnp.maximum(clash, same.astype(I32))
    for k in (1, 2, 4):
        clash = jnp.maximum(clash, jnp.where(within >= k, pltpu.roll(clash, k, 1), 0))
    meta = place + kind1 * 16384 + clash * (1 << 20)
    meta_ref[...] = jnp.where(lane < CAP, meta, counts)

    @pl.loop(0, OWNED // 128)
    def _(i):
        srcf[pl.ds(pl.multiple_of(i * 128, 128), 128), :] = src_ref[
            pl.ds(pl.multiple_of(i * 128, 128), 128), :
        ].astype(F32)

    @pl.loop(0, SLOTS // 128)
    def _(i):
        sendf[pl.ds(pl.multiple_of(i * 128, 128), 128), :] = jnp.zeros((128, 128), F32)

    copy.wait()

    for j in range(OWNED // 128):

        @pl.loop(0, 8)
        def _(i):
            for u in range(16):
                n = i * 16 + u
                sendf[pl.ds(slot_s[j, n], 1), :] = srcf[pl.ds(j * 128 + n, 1), :]

    @pl.loop(0, SLOTS // 128)
    def _(i):
        rows = pl.ds(pl.multiple_of(i * 128, 128), 128)
        send_ref[rows, :] = sendf[rows, :].astype(BF16)


def partners():
    tx, ty = lax.axis_index("tx"), lax.axis_index("ty")

    def to(k):
        return (tx + k % NX_DEV) % NX_DEV, (ty + k // NX_DEV) % NY_DEV

    def back(k):
        return (tx + NX_DEV - k % NX_DEV) % NX_DEV, (ty + NY_DEV - k // NX_DEV) % NY_DEV

    return tx, ty, to, back


def greet_all(to):
    barrier = pltpu.get_barrier_semaphore()

    @pl.loop(1, DEV)
    def _(k):
        pl.semaphore_signal(barrier, inc=1, device_id=to(k), device_id_type=MESH)

    return barrier


def forward_kernel(
    send_ref, msend_ref, spread_ref,
    seed_ref, idx_ref, meta_ref,
    recv, mid, mid2, last, kcol,
    ssem, rsem, xs, xr, ys, yr, lsem,
):
    tx, ty, to, back = partners()
    me_t, me_q = tx * NY_DEV + ty, ty * NX_DEV + tx
    barrier = greet_all(to)
    own = pltpu.make_async_copy(send_ref.at[me_t], recv.at[me_q], lsem.at[0])
    own.start()
    own_mid = pltpu.make_async_copy(msend_ref.at[tx], mid.at[tx], lsem.at[1])
    own_mid.start()
    pl.semaphore_wait(barrier, DEV - 1)

    def x_copy(i, peer, there):
        return pltpu.make_async_remote_copy(
            src_ref=msend_ref.at[peer], dst_ref=mid.at[there], send_sem=xs.at[i],
            recv_sem=xr.at[i], device_id=(peer, ty), device_id_type=MESH,
        )

    def y_copy(i, peer, there):
        return pltpu.make_async_remote_copy(
            src_ref=mid2.at[peer], dst_ref=last.at[there], send_sem=ys.at[i],
            recv_sem=yr.at[i], device_id=(tx, peer), device_id_type=MESH,
        )

    def d_copy(k, peer, there):
        return pltpu.make_async_remote_copy(
            src_ref=send_ref.at[peer[0] * NY_DEV + peer[1]], dst_ref=recv.at[there],
            send_sem=ssem.at[k], recv_sem=rsem.at[k], device_id=peer, device_id_type=MESH,
        )

    @pl.loop(1, NX_DEV)
    def _(i):
        x_copy(i, (tx + i) % NX_DEV, tx).start()

    @pl.loop(1, 48)
    def _(k):
        d_copy(k, to(k), me_q).start()

    own_mid.wait()

    @pl.loop(1, NX_DEV)
    def _(i):
        x_copy(i, (tx + NX_DEV - i) % NX_DEV, (tx + NX_DEV - i) % NX_DEV).wait()

    for j in range(NY_DEV):
        mid2[j] = mid[:, j, :]
    own_meta = pltpu.make_async_copy(mid2.at[ty], last.at[ty], lsem.at[2])
    own_meta.start()

    @pl.loop(1, NY_DEV)
    def _(i):
        y_copy(i, (ty + i) % NY_DEV, ty).start()

    @pl.loop(48, DEV)
    def _(k):
        d_copy(k, to(k), me_q).start()

    own_meta.wait()
    own.wait()

    @pl.loop(1, NY_DEV)
    def _(i):
        y_copy(i, (ty + NY_DEV - i) % NY_DEV, (ty + NY_DEV - i) % NY_DEV).wait()

    meta = last[...].reshape(DEV, 128)
    meta_ref[...] = meta
    idx_ref[...] = meta & 16383
    kind1 = jnp.transpose(((meta >> 14) & 31).astype(F32))[:CAP, :]
    kcol[...] = kind1

    @pl.loop(0, NY_DEV)
    def _(g):
        @pl.loop(0, NX_DEV)
        def _(i):
            k = g * NX_DEV + i

            @pl.when(k > 0)
            def _():
                a, b = back(k)
                d_copy(k, (a, b), b * NX_DEV + a).wait()

        q = (ty + NY_DEV - g) % NY_DEV
        kinds = pltpu.roll(kcol[...], (DEV - q * NX_DEV) % DEV, 1)
        kb = jnp.concatenate(
            [jnp.broadcast_to(kinds[:, i : i + 1], (CAP, 128)) for i in range(NX_DEV)], axis=0
        ).astype(BF16)
        x = recv[pl.ds(q * NX_DEV, NX_DEV)].reshape(NX_DEV * CAP, 128)
        zero = jnp.zeros_like(x)
        masked = jnp.concatenate(
            [jnp.where(kb == jnp.asarray(k + 1, BF16), x, zero) for k in range(KINDS)], axis=1
        )
        rows = pl.ds(pl.multiple_of(q * (NX_DEV * CAP), NX_DEV * CAP), NX_DEV * CAP)
        seed_ref[rows, :] = dot(masked, spread_ref[...])


def scatter_kernel(idx_s, meta_s, seed_ref, cot_ref, rhs_ref, sem):
    def load(n):
        c, l = n // NZ, n % NZ
        return pltpu.make_async_copy(
            cot_ref.at[l, :, pl.ds(pl.multiple_of(c * 128, 128), 128)],
            rhs_ref.at[pl.ds(pl.multiple_of(n * CX, CX), CX), :],
            sem.at[n],
        )

    @pl.loop(0, CH * NZ)
    def _(n):
        load(n).start()

    rhs_ref[pl.ds(PATCHES, CAP), :] = jnp.zeros((CAP, 128), F32)

    @pl.loop(0, CH * NZ)
    def _(n):
        load(n).wait()

    @pl.loop(0, DEV)
    def _(q):
        count = meta_s[q, CAP]
        for g in range(CAP // GROUP):

            @pl.when(count > g * GROUP)
            def _():
                base = pl.multiple_of(q * CAP + g * GROUP, GROUP)
                at = [pl.ds(idx_s[q, g * GROUP + u], 1) for u in range(GROUP)]
                clash = meta_s[q, g * GROUP + GROUP - 1] >> 20

                @pl.when(clash == 0)
                def _():
                    new = [rhs_ref[at[u], :] + seed_ref[pl.ds(base + u, 1), :] for u in range(GROUP)]
                    for u in range(GROUP):
                        rhs_ref[at[u], :] = new[u]

                @pl.when(clash != 0)
                def _():
                    for u in range(GROUP):
                        rhs_ref[at[u], :] = rhs_ref[at[u], :] + seed_ref[pl.ds(base + u, 1), :]


def backward_kernel(
    idx_s, slot_s, rhs_ref, cond_ref, diag_ref, kb_ref, spread_ref, deriv_ref,
    out_ref, grad_ref,
    cond, inv, g0, g1, adj, heat, hsend, recv, recvf, pulled,
    xe, ye, xh, yh,
    ssem, rsem, hs, hr, fsem, osem, lsem,
):
    tx, ty, to, back = partners()
    me_t, me_q = tx * NY_DEV + ty, ty * NX_DEV + tx
    lane = iota((8, 128), 1)

    def plane(field, buffer, n, s):
        c, l = n // NZ, n % NZ
        return (
            field.at[l, :, pl.ds(pl.multiple_of(c * 128, 128), 128)],
            buffer.at[pl.ds(pl.multiple_of(n * CX, CX), CX), :],
            s,
        )

    def load(n, which):
        return pltpu.make_async_copy(
            *plane((cond_ref, diag_ref)[which], (cond, inv)[which], n, fsem.at[which, n])
        )

    def save(n):
        hbm, vmem, s = plane(out_ref, adj, n, osem.at[n])
        return pltpu.make_async_copy(vmem, hbm, s)

    @pl.loop(0, CH * NZ)
    def _(n):
        load(n, 0).start()
        load(n, 1).start()

    barrier = greet_all(to)
    adj[pl.ds(PATCHES, CAP), :] = jnp.zeros((CAP, 128), F32)
    for g in (g0, g1):
        for c in range(CH):
            for l in (0, NZ + 1):

                @pl.loop(0, SEG // 16)
                def _(i):
                    g[pl.ds((c * (NZ + 2) + l) * SEG + i * 16, 16), :] = jnp.zeros((16, 128), F32)

    @pl.loop(0, CH * NZ)
    def _(n):
        load(n, 0).wait()
        load(n, 1).wait()

    def row_of(c, l, r):
        return pl.multiple_of(c * (NZ * CX) + l * CX + r, 8)

    def grow_of(c, l, r):
        return pl.multiple_of((c * (NZ + 2) + l + 1) * SEG + 8 + r, 8)

    def edges(acc, lo, hi, j):
        left, right = acc
        left = jnp.where(lane == j, pltpu.roll(lo, j, 1), left)
        right = jnp.where(lane == j, pltpu.roll(hi, (j + 1) % 128, 1), right)
        return left, right

    def visit(body, after=None):
        for h in range(2):

            def step(i, acc):
                for u in range(2):
                    j = i * 2 + u
                    lo, hi = body(h * 4 + j // 32, (j % 32) * 8, j, h)
                    if after is not None:
                        acc = edges(acc, lo, hi, j)
                return acc

            acc = lax.fori_loop(0, 64, step, (jnp.zeros((8, 128), F32),) * 2)
            if after is not None:
                after(h, acc)

    def keep_edges(s):
        def after(h, acc):
            ye[s, 0, pl.ds(h * 8, 8), :] = acc[0]
            ye[s, 1, pl.ds(h * 8, 8), :] = acc[1]

        return after

    def start(l, r, j, h):
        ends = []
        for c in range(CH):
            at = pl.ds(row_of(c, l, r), 8)
            q = 1.0 / inv[at, :]
            inv[at, :] = q
            g = cond[at, :] * (rhs_ref[at, :] * q)
            g0[pl.ds(grow_of(c, l, r), 8), :] = g
            ends.append(g)
        return ends[0], ends[-1]

    def sums(g, s, l, r, j, h):
        own = [g[pl.ds(grow_of(c, l, r), 8), :] for c in range(CH)]
        before = pltpu.roll(yh[s, 0, pl.ds(h * 8, 8), :], 127 - j, 1)
        behind = pltpu.roll(yh[s, 1, pl.ds(h * 8, 8), :], (128 - j) % 128, 1)
        wide = [before, *own, behind]
        out = []
        for c in range(CH):
            b = grow_of(c, l, r)
            west = pltpu.roll(jnp.where(lane == 127, wide[c], own[c]), 1, 1)
            east = pltpu.roll(jnp.where(lane == 0, wide[c + 2], own[c]), 127, 1)
            total = g[pl.ds(b - 1, 8), :] + g[pl.ds(b + 1, 8), :]
            total = total + west + east
            out.append(total + g[pl.ds(b - SEG, 8), :] + g[pl.ds(b + SEG, 8), :])
        return out

    def first(l, r, j, h):
        ends = []
        for c, total in enumerate(sums(g0, 0, l, r, j, h)):
            at = pl.ds(row_of(c, l, r), 8)
            g = cond[at, :] * ((rhs_ref[at, :] + total) * inv[at, :])
            g1[pl.ds(grow_of(c, l, r), 8), :] = g
            ends.append(g)
        return ends[0], ends[-1]

    def second(l, r, j, h):
        for c, total in enumerate(sums(g1, 1, l, r, j, h)):
            at = pl.ds(row_of(c, l, r), 8)
            adj[at, :] = (rhs_ref[at, :] + total) * inv[at, :]
        return None, None

    up, down = (tx + NX_DEV - 1) % NX_DEV, (tx + 1) % NX_DEV
    west, east = (ty + NY_DEV - 1) % NY_DEV, (ty + 1) % NY_DEV

    def halo(s, g):
        for c in range(CH):
            for l in range(NZ):
                n = c * NZ + l
                b = (c * (NZ + 2) + l + 1) * SEG + 8
                xe[s, 0, n : n + 1, :] = g[b : b + 1, :]
                xe[s, 1, n : n + 1, :] = g[b + CX - 1 : b + CX, :]
        if s == 0:
            pl.semaphore_wait(barrier, DEV - 1)
        copies = []
        for i, (src, dst, dev) in enumerate(
            (
                (ye.at[s, 0], yh.at[s, 1], (tx, west)),
                (ye.at[s, 1], yh.at[s, 0], (tx, east)),
                (xe.at[s, 0], xh.at[s, 1], (up, ty)),
                (xe.at[s, 1], xh.at[s, 0], (down, ty)),
            )
        ):
            copies.append(
                pltpu.make_async_remote_copy(
                    src_ref=src, dst_ref=dst, send_sem=hs.at[s, i], recv_sem=hr.at[s, i],
                    device_id=dev, device_id_type=MESH,
                )
            )
            copies[-1].start()
        for copy in copies:
            copy.wait()
        outer = jnp.where(tx == 0, 0.0, xh[s, 0])
        outer2 = jnp.where(tx == NX_DEV - 1, 0.0, xh[s, 1])
        for c in range(CH):
            for l in range(NZ):
                n = c * NZ + l
                b = (c * (NZ + 2) + l + 1) * SEG + 8
                g[b - 1 : b, :] = outer[n : n + 1, :]
                g[b + CX : b + CX + 1, :] = outer2[n : n + 1, :]
        yh[s, 0] = jnp.where(ty == 0, 0.0, yh[s, 0])
        yh[s, 1] = jnp.where(ty == NY_DEV - 1, 0.0, yh[s, 1])

    visit(start, keep_edges(0))
    halo(0, g0)
    visit(first, keep_edges(1))
    halo(1, g1)
    visit(second)

    @pl.loop(0, CH * NZ)
    def _(n):
        save(n).start()

    def take(q):
        for u in range(CAP):
            heat[pl.ds(u, 1), :] = adj[pl.ds(idx_s[q, u], 1), :]
        hsend[q] = heat[...].astype(BF16)

    def d_copy(k, peer, there):
        return pltpu.make_async_remote_copy(
            src_ref=hsend.at[peer[1] * NX_DEV + peer[0]], dst_ref=recv.at[there],
            send_sem=ssem.at[k], recv_sem=rsem.at[k], device_id=peer, device_id_type=MESH,
        )

    @pl.loop(1, DEV)
    def _(k):
        a, b = to(k)
        take(b * NX_DEV + a)
        d_copy(k, (a, b), me_t).start()

    take(me_q)
    own = pltpu.make_async_copy(hsend.at[me_q], recv.at[me_t], lsem)
    own.start()

    @pl.loop(0, CH * NZ)
    def _(n):
        save(n).wait()

    own.wait()

    @pl.loop(1, DEV)
    def _(k):
        a, b = back(k)
        d_copy(k, (a, b), a * NY_DEV + b).wait()

    @pl.loop(0, DEV // 4)
    def _(i):
        recvf[pl.ds(pl.multiple_of(i * 128, 128), 128), :] = (
            recv[pl.ds(i * 4, 4)].reshape(128, 128).astype(F32)
        )

    @pl.loop(0, 8)
    def _(i):
        for j in range(2):

            @pl.loop(0, 8)
            def _(v):
                for u in range(16):
                    n = v * 16 + u
                    pulled[pl.ds(j * 128 + n, 1), :] = recvf[pl.ds(slot_s[i * 2 + j, n], 1), :]

        rows = pl.ds(pl.multiple_of(i * 256, 256), 256)
        x = pulled[...].astype(BF16)
        kb = kb_ref[rows, :]
        zero = jnp.zeros_like(x)
        masked = jnp.concatenate(
            [jnp.where(kb == jnp.asarray(k, BF16), x, zero) for k in range(KINDS)], axis=1
        )
        grad_ref[rows, :] = deriv_ref[rows, :] * dot(masked, spread_ref[...])


def local(cot_field, conductance, diagonal, source_adjoint, spreading, heat_deriv, block_tile, block_patch, block_kind):
    grid16 = (OWNED // 128, 128)
    shape = jax.ShapeDtypeStruct
    send, meta, slots, kinds = pl.pallas_call(
        route_kernel,
        out_shape=(
            shape((SLOTS, 128), BF16),
            shape((DEV, 128), I32),
            shape(grid16, I32),
            shape((OWNED, 128), BF16),
        ),
        in_specs=[VMEM] * 4,
        out_specs=(VMEM,) * 4,
        scratch_shapes=[
            pltpu.VMEM((OWNED, 128), F32),
            pltpu.VMEM((SLOTS, 128), F32),
            pltpu.SMEM(grid16, I32),
            pltpu.SemaphoreType.DMA,
        ],
        compiler_params=pltpu.CompilerParams(vmem_limit_bytes=20 << 20),
        name="route",
    )(block_tile.reshape(grid16), block_patch.reshape(grid16), block_kind.reshape(grid16), source_adjoint)

    dma = pltpu.SemaphoreType.DMA
    seeds, idx, got = pl.pallas_call(
        forward_kernel,
        out_shape=(shape((SLOTS, 128), F32), shape((DEV, 128), I32), shape((DEV, 128), I32)),
        in_specs=[VMEM] * 3,
        out_specs=(VMEM,) * 3,
        scratch_shapes=[
            pltpu.VMEM((DEV, CAP, 128), BF16),
            pltpu.VMEM((NX_DEV, NY_DEV, 128), I32),
            pltpu.VMEM((NY_DEV, NX_DEV, 128), I32),
            pltpu.VMEM((NY_DEV, NX_DEV, 128), I32),
            pltpu.VMEM((CAP, DEV), F32),
            dma((DEV,)),
            dma((DEV,)),
            dma((NX_DEV,)),
            dma((NX_DEV,)),
            dma((NY_DEV,)),
            dma((NY_DEV,)),
            dma((3,)),
        ],
        compiler_params=pltpu.CompilerParams(
            collective_id=0, has_side_effects=True, vmem_limit_bytes=24 << 20
        ),
        name="forward",
    )(
        send.reshape(DEV, CAP, 128),
        meta.reshape(NX_DEV, NY_DEV, 128),
        spreading.reshape(KINDS * 128, 128),
    )

    rhs = pl.pallas_call(
        scatter_kernel,
        out_shape=shape((ROWS, 128), F32),
        in_specs=[SMEM, SMEM, VMEM, ANY],
        out_specs=VMEM,
        scratch_shapes=[dma((CH * NZ,))],
        compiler_params=pltpu.CompilerParams(vmem_limit_bytes=24 << 20),
        name="scatter",
    )(idx, got, seeds, cot_field)

    spread_t = jnp.swapaxes(spreading, 1, 2).reshape(KINDS * 128, 128)
    flat = pltpu.VMEM((PATCHES, 128), F32)
    padded = pltpu.VMEM((GROWS, 128), F32)
    temp, grad = pl.pallas_call(
        backward_kernel,
        out_shape=(shape(cot_field.shape, F32), shape((OWNED, 128), F32)),
        in_specs=[SMEM, SMEM, VMEM, ANY, ANY, VMEM, VMEM, VMEM],
        out_specs=(ANY, VMEM),
        scratch_shapes=[
            flat,
            flat,
            padded,
            padded,
            pltpu.VMEM((ROWS, 128), F32),
            pltpu.VMEM((CAP, 128), F32),
            pltpu.VMEM((DEV, CAP, 128), BF16),
            pltpu.VMEM((DEV, CAP, 128), BF16),
            pltpu.VMEM((SLOTS, 128), F32),
            pltpu.VMEM((256, 128), F32),
            pltpu.VMEM((2, 2, CH * NZ, 128), F32),
            pltpu.VMEM((2, 2, 16, 128), F32),
            pltpu.VMEM((2, 2, CH * NZ, 128), F32),
            pltpu.VMEM((2, 2, 16, 128), F32),
            dma((DEV,)),
            dma((DEV,)),
            dma((2, 4)),
            dma((2, 4)),
            dma((2, CH * NZ)),
            dma((CH * NZ,)),
            dma,
        ],
        compiler_params=pltpu.CompilerParams(
            collective_id=1, has_side_effects=True, vmem_limit_bytes=58 << 20
        ),
        name="backward",
    )(idx, slots, rhs, conductance, diagonal, kinds, spread_t, heat_deriv)
    return temp, grad


def solution(mesh):
    blocks = P(("tx", "ty"))
    field = P(None, "tx", "ty")
    in_specs = (
        field, field, field, P(("tx", "ty"), None), P(), P(("tx", "ty"), None),
        P(("tx", "ty"), None), blocks, blocks,
    )
    out_specs = (field, P(("tx", "ty"), None))
    return jax.shard_map(local, mesh=mesh, in_specs=in_specs, out_specs=out_specs, check_vma=False)
```

```python
import functools

import jax
import jax.numpy as jnp
from jax import lax
from jax.experimental import pallas as pl
from jax.experimental.pallas import tpu as pltpu
from jax.sharding import PartitionSpec as P

NX_DEV, NY_DEV = 8, 16
DEV = NX_DEV * NY_DEV
CAP = 32
SLOTS = DEV * CAP
KINDS = 16
NZ, CX, CY = 8, 256, 512
CH = CY // 128
PATCHES = NZ * CX * CH
ROWS = PATCHES + CAP
SEG = CX + 16
GROWS = CH * (NZ + 2) * SEG
OWNED = 2048
GROUP = 8
UNROLL, BATCH = 16, 1
F32, BF16, I32 = jnp.float32, jnp.bfloat16, jnp.int32
MESH = pl.DeviceIdType.MESH
VMEM = pl.BlockSpec(memory_space=pltpu.VMEM)
SMEM = pl.BlockSpec(memory_space=pltpu.SMEM)
ANY = pl.BlockSpec(memory_space=pl.ANY)
NT = (((1,), (1,)), ((), ()))


def dot(a, b):
    return jnp.dot(a, b, preferred_element_type=F32)


def iota(shape, dim):
    return lax.broadcasted_iota(I32, shape, dim)


def route_kernel(
    table_ref, src_ref,
    send_ref, meta_ref, slot_ref, kb_ref,
    srcf, sendf, slot_s, sem,
):
    sub, lane = iota((128, 128), 0), iota((128, 128), 1)
    before = (sub < lane).astype(F32).astype(BF16)
    ones = jnp.ones((128, 128), BF16)
    rank_row = iota((CAP, 128), 0)
    count = jnp.zeros((128, 128), F32)
    table = jnp.zeros((128, 128), F32)
    for j in range(OWNED // 128):
        tile, patch, kind = (table_ref[n * 16 + j : n * 16 + j + 1, :] for n in range(3))
        place = (patch & (CH - 1)) * (NZ * CX) + (patch >> 2)
        hit = (sub == tile).astype(F32)
        hit16 = hit.astype(BF16)
        rank = jnp.sum(hit * (dot(hit16, before) + count), axis=0, keepdims=True).astype(I32)
        count = count + dot(hit16, ones)
        slot_ref[j : j + 1, :] = tile * CAP + rank
        at = (rank_row == rank).astype(F32)
        parts = jnp.concatenate(
            [
                at * (place >> 7).astype(F32),
                at * (place & 127).astype(F32),
                at * (kind + 1).astype(F32),
                jnp.zeros((128 - 3 * CAP, 128), F32),
            ],
            axis=0,
        ).astype(BF16)
        table = table + lax.dot_general(hit16, parts, NT, preferred_element_type=F32)
        kb_ref[pl.ds(j * 128, 128), :] = jnp.transpose(
            jnp.broadcast_to(kind.astype(F32), (128, 128))
        ).astype(BF16)
    copy = pltpu.make_async_copy(slot_ref, slot_s, sem)
    copy.start()
    counts = count.astype(I32)
    place = (table * 128.0 + pltpu.roll(table, 128 - CAP, 1)).astype(I32)
    kind1 = pltpu.roll(table, 128 - 2 * CAP, 1).astype(I32)
    place = jnp.where(lane < counts, place, PATCHES + lane)
    within = lane & (GROUP - 1)
    clash = jnp.zeros((128, 128), I32)
    for k in range(1, GROUP):
        same = (pltpu.roll(place, k, 1) == place) & (within >= k)
        clash = jnp.maximum(clash, same.astype(I32))
    for k in (1, 2, 4):
        clash = jnp.maximum(clash, jnp.where(within >= k, pltpu.roll(clash, k, 1), 0))
    meta = place + kind1 * 16384 + clash * (1 << 20)
    meta_ref[...] = jnp.where(lane < CAP, meta, counts)

    @pl.loop(0, OWNED // 128)
    def _(i):
        srcf[pl.ds(pl.multiple_of(i * 128, 128), 128), :] = src_ref[
            pl.ds(pl.multiple_of(i * 128, 128), 128), :
        ].astype(F32)

    @pl.loop(0, SLOTS // 128)
    def _(i):
        sendf[pl.ds(pl.multiple_of(i * 128, 128), 128), :] = jnp.zeros((128, 128), F32)

    copy.wait()

    for j in range(OWNED // 128):

        @pl.loop(0, 8)
        def _(i):
            for u in range(16):
                n = i * 16 + u
                sendf[pl.ds(slot_s[j, n], 1), :] = srcf[pl.ds(j * 128 + n, 1), :]

    @pl.loop(0, SLOTS // 128)
    def _(i):
        rows = pl.ds(pl.multiple_of(i * 128, 128), 128)
        send_ref[rows, :] = sendf[rows, :].astype(BF16)


def partners():
    tx, ty = lax.axis_index("tx"), lax.axis_index("ty")

    def to(k):
        return (tx + k % NX_DEV) % NX_DEV, (ty + k // NX_DEV) % NY_DEV

    def back(k):
        return (tx + NX_DEV - k % NX_DEV) % NX_DEV, (ty + NY_DEV - k // NX_DEV) % NY_DEV

    return tx, ty, to, back


def greet_all(to):
    barrier = pltpu.get_barrier_semaphore()

    @pl.loop(1, DEV)
    def _(k):
        pl.semaphore_signal(barrier, inc=1, device_id=to(k), device_id_type=MESH)

    return barrier


def forward_kernel(
    send_ref, msend_ref, spread_ref,
    seed_ref, idx_ref, meta_ref,
    recv, mid, mid2, last, kcol,
    ssem, rsem, xs, xr, ys, yr, lsem,
):
    tx, ty, to, back = partners()
    me_t, me_q = tx * NY_DEV + ty, ty * NX_DEV + tx
    barrier = greet_all(to)
    own = pltpu.make_async_copy(send_ref.at[me_t], recv.at[me_q], lsem.at[0])
    own.start()
    own_mid = pltpu.make_async_copy(msend_ref.at[tx], mid.at[tx], lsem.at[1])
    own_mid.start()
    pl.semaphore_wait(barrier, DEV - 1)

    def x_copy(i, peer, there):
        return pltpu.make_async_remote_copy(
            src_ref=msend_ref.at[peer], dst_ref=mid.at[there], send_sem=xs.at[i],
            recv_sem=xr.at[i], device_id=(peer, ty), device_id_type=MESH,
        )

    def y_copy(i, peer, there):
        return pltpu.make_async_remote_copy(
            src_ref=mid2.at[peer], dst_ref=last.at[there], send_sem=ys.at[i],
            recv_sem=yr.at[i], device_id=(tx, peer), device_id_type=MESH,
        )

    def d_copy(k, peer, there):
        return pltpu.make_async_remote_copy(
            src_ref=send_ref.at[peer[0] * NY_DEV + peer[1]], dst_ref=recv.at[there],
            send_sem=ssem.at[k], recv_sem=rsem.at[k], device_id=peer, device_id_type=MESH,
        )

    @pl.loop(1, NX_DEV)
    def _(i):
        x_copy(i, (tx + i) % NX_DEV, tx).start()

    @pl.loop(1, 48)
    def _(k):
        d_copy(k, to(k), me_q).start()

    own_mid.wait()

    @pl.loop(1, NX_DEV)
    def _(i):
        x_copy(i, (tx + NX_DEV - i) % NX_DEV, (tx + NX_DEV - i) % NX_DEV).wait()

    for j in range(NY_DEV):
        mid2[j] = mid[:, j, :]
    own_meta = pltpu.make_async_copy(mid2.at[ty], last.at[ty], lsem.at[2])
    own_meta.start()

    @pl.loop(1, NY_DEV)
    def _(i):
        y_copy(i, (ty + i) % NY_DEV, ty).start()

    @pl.loop(48, DEV)
    def _(k):
        d_copy(k, to(k), me_q).start()

    own_meta.wait()
    own.wait()

    @pl.loop(1, NY_DEV)
    def _(i):
        y_copy(i, (ty + NY_DEV - i) % NY_DEV, (ty + NY_DEV - i) % NY_DEV).wait()

    meta = last[...].reshape(DEV, 128)
    meta_ref[...] = meta
    idx_ref[...] = meta & 16383
    kind1 = jnp.transpose(((meta >> 14) & 31).astype(F32))[:CAP, :]
    kcol[...] = kind1

    @pl.loop(0, NY_DEV)
    def _(g):
        @pl.loop(0, NX_DEV)
        def _(i):
            k = g * NX_DEV + i

            @pl.when(k > 0)
            def _():
                a, b = back(k)
                d_copy(k, (a, b), b * NX_DEV + a).wait()

        q = (ty + NY_DEV - g) % NY_DEV
        kinds = pltpu.roll(kcol[...], (DEV - q * NX_DEV) % DEV, 1)
        kb = jnp.concatenate(
            [jnp.broadcast_to(kinds[:, i : i + 1], (CAP, 128)) for i in range(NX_DEV)], axis=0
        ).astype(BF16)
        x = recv[pl.ds(q * NX_DEV, NX_DEV)].reshape(NX_DEV * CAP, 128)
        zero = jnp.zeros_like(x)
        masked = jnp.concatenate(
            [jnp.where(kb == jnp.asarray(k + 1, BF16), x, zero) for k in range(KINDS)], axis=1
        )
        rows = pl.ds(pl.multiple_of(q * (NX_DEV * CAP), NX_DEV * CAP), NX_DEV * CAP)
        seed_ref[rows, :] = dot(masked, spread_ref[...])


def scatter_kernel(idx_s, meta_s, seed_ref, cot_ref, rhs_ref, sem):
    def load(n):
        c, l = n // NZ, n % NZ
        return pltpu.make_async_copy(
            cot_ref.at[l, :, pl.ds(pl.multiple_of(c * 128, 128), 128)],
            rhs_ref.at[pl.ds(pl.multiple_of(n * CX, CX), CX), :],
            sem.at[n],
        )

    @pl.loop(0, CH * NZ)
    def _(n):
        load(n).start()

    rhs_ref[pl.ds(PATCHES, CAP), :] = jnp.zeros((CAP, 128), F32)

    @pl.loop(0, CH * NZ)
    def _(n):
        load(n).wait()

    @pl.loop(0, DEV)
    def _(q):
        count = meta_s[q, CAP]
        for g in range(CAP // GROUP):

            @pl.when(count > g * GROUP)
            def _():
                base = pl.multiple_of(q * CAP + g * GROUP, GROUP)
                at = [pl.ds(idx_s[q, g * GROUP + u], 1) for u in range(GROUP)]
                clash = meta_s[q, g * GROUP + GROUP - 1] >> 20

                @pl.when(clash == 0)
                def _():
                    new = [rhs_ref[at[u], :] + seed_ref[pl.ds(base + u, 1), :] for u in range(GROUP)]
                    for u in range(GROUP):
                        rhs_ref[at[u], :] = new[u]

                @pl.when(clash != 0)
                def _():
                    for u in range(GROUP):
                        rhs_ref[at[u], :] = rhs_ref[at[u], :] + seed_ref[pl.ds(base + u, 1), :]


def backward_kernel(
    idx_s, slot_s, rhs_ref, cond_ref, diag_ref, kb_ref, spread_ref, deriv_ref,
    out_ref, grad_ref,
    inv, g0, g1, adj, heat, hsend, recv, recvf, pulled,
    xe, ye, xh, yh,
    ssem, rsem, hs, hr, lsem,
):
    tx, ty, to, back = partners()
    me_t, me_q = tx * NY_DEV + ty, ty * NX_DEV + tx
    lane = iota((8, 128), 1)
    barrier = greet_all(to)
    adj[pl.ds(PATCHES, CAP), :] = jnp.zeros((CAP, 128), F32)
    for g in (g0, g1):
        for c in range(CH):
            for l in (0, NZ + 1):

                @pl.loop(0, CX // 64)
                def _(i):
                    g[pl.ds((c * (NZ + 2) + l) * SEG + 8 + i * 64, 64), :] = jnp.zeros((64, 128), F32)

    def cell(c, l, r):
        return l, pl.ds(r, 8), pl.ds(c * 128, 128)

    def row_of(c, l, r):
        return pl.ds(pl.multiple_of(c * (NZ * CX) + l * CX + r, 8), 8)

    def grow_of(c, l, r):
        return pl.multiple_of((c * (NZ + 2) + l + 1) * SEG + 8 + r, 8)

    def edges(acc, lo, hi, j):
        left, right = acc
        left = jnp.where(lane == j, pltpu.roll(lo, j, 1), left)
        right = jnp.where(lane == j, pltpu.roll(hi, (j + 1) % 128, 1), right)
        return left, right

    def visit(body, after=None):
        for h in range(2):

            def step(i, acc):
                for v in range(0, UNROLL, BATCH):
                    stores = []
                    for u in range(v, v + BATCH):
                        j = i * UNROLL + u
                        r = pl.multiple_of((i % (32 // UNROLL)) * (UNROLL * 8), 8) + u * 8
                        writes, lo, hi = body(h * 4 + i // (32 // UNROLL), r, j, h)
                        stores += writes
                        if after is not None:
                            acc = edges(acc, lo, hi, j)
                    for ref, at, value in stores:
                        ref[at] = value
                return acc

            acc = lax.fori_loop(0, 128 // UNROLL, step, (jnp.zeros((8, 128), F32),) * 2)
            if after is not None:
                after(h, acc)

    def keep_edges(s):
        def after(h, acc):
            ye[s, 0, pl.ds(h * 8, 8), :] = acc[0]
            ye[s, 1, pl.ds(h * 8, 8), :] = acc[1]

        return after

    def start(l, r, j, h):
        writes, ends = [], []
        for c in range(CH):
            q = 1.0 / diag_ref[cell(c, l, r)]
            g = cond_ref[cell(c, l, r)] * (rhs_ref[row_of(c, l, r), :] * q)
            writes.append((inv, (row_of(c, l, r), slice(None)), q))
            writes.append((g0, (pl.ds(grow_of(c, l, r), 8), slice(None)), g))
            ends.append(g)
        return writes, ends[0], ends[-1]

    def sums(g, s, l, r, j, h):
        own = [g[pl.ds(grow_of(c, l, r), 8), :] for c in range(CH)]
        before = pltpu.roll(yh[s, 0, pl.ds(h * 8, 8), :], 127 - j, 1)
        behind = pltpu.roll(yh[s, 1, pl.ds(h * 8, 8), :], (128 - j) % 128, 1)
        wide = [before, *own, behind]
        out = []
        for c in range(CH):
            b = grow_of(c, l, r)
            west = pltpu.roll(jnp.where(lane == 127, wide[c], own[c]), 1, 1)
            east = pltpu.roll(jnp.where(lane == 0, wide[c + 2], own[c]), 127, 1)
            total = g[pl.ds(b - 1, 8), :] + g[pl.ds(b + 1, 8), :]
            total = total + west + east
            out.append(total + g[pl.ds(b - SEG, 8), :] + g[pl.ds(b + SEG, 8), :])
        return out

    def first(l, r, j, h):
        writes, ends = [], []
        for c, total in enumerate(sums(g0, 0, l, r, j, h)):
            at = row_of(c, l, r), slice(None)
            g = cond_ref[cell(c, l, r)] * ((rhs_ref[at] + total) * inv[at])
            writes.append((g1, (pl.ds(grow_of(c, l, r), 8), slice(None)), g))
            ends.append(g)
        return writes, ends[0], ends[-1]

    def second(l, r, j, h):
        writes = []
        for c, total in enumerate(sums(g1, 1, l, r, j, h)):
            at = row_of(c, l, r), slice(None)
            value = (rhs_ref[at] + total) * inv[at]
            writes.append((adj, at, value))
            writes.append((out_ref, cell(c, l, r), value))
        return writes, None, None

    up, down = (tx + NX_DEV - 1) % NX_DEV, (tx + 1) % NX_DEV
    west, east = (ty + NY_DEV - 1) % NY_DEV, (ty + 1) % NY_DEV

    def halo(s, g):
        for c in range(CH):
            for l in range(NZ):
                n = c * NZ + l
                b = (c * (NZ + 2) + l + 1) * SEG + 8
                xe[s, 0, n : n + 1, :] = g[b : b + 1, :]
                xe[s, 1, n : n + 1, :] = g[b + CX - 1 : b + CX, :]
        if s == 0:
            pl.semaphore_wait(barrier, DEV - 1)
        copies = []
        for i, (src, dst, dev) in enumerate(
            (
                (ye.at[s, 0], yh.at[s, 1], (tx, west)),
                (ye.at[s, 1], yh.at[s, 0], (tx, east)),
                (xe.at[s, 0], xh.at[s, 1], (up, ty)),
                (xe.at[s, 1], xh.at[s, 0], (down, ty)),
            )
        ):
            copies.append(
                pltpu.make_async_remote_copy(
                    src_ref=src, dst_ref=dst, send_sem=hs.at[s, i], recv_sem=hr.at[s, i],
                    device_id=dev, device_id_type=MESH,
                )
            )
            copies[-1].start()
        for copy in copies:
            copy.wait()
        outer = jnp.where(tx == 0, 0.0, xh[s, 0])
        outer2 = jnp.where(tx == NX_DEV - 1, 0.0, xh[s, 1])
        for c in range(CH):
            for l in range(NZ):
                n = c * NZ + l
                b = (c * (NZ + 2) + l + 1) * SEG + 8
                g[b - 1 : b, :] = outer[n : n + 1, :]
                g[b + CX : b + CX + 1, :] = outer2[n : n + 1, :]
        yh[s, 0] = jnp.where(ty == 0, 0.0, yh[s, 0])
        yh[s, 1] = jnp.where(ty == NY_DEV - 1, 0.0, yh[s, 1])

    visit(start, keep_edges(0))
    halo(0, g0)
    visit(first, keep_edges(1))
    halo(1, g1)
    visit(second)

    def take(q):
        for u in range(CAP):
            heat[pl.ds(u, 1), :] = adj[pl.ds(idx_s[q, u], 1), :]
        hsend[q] = heat[...].astype(BF16)

    def d_copy(k, peer, there):
        return pltpu.make_async_remote_copy(
            src_ref=hsend.at[peer[1] * NX_DEV + peer[0]], dst_ref=recv.at[there],
            send_sem=ssem.at[k], recv_sem=rsem.at[k], device_id=peer, device_id_type=MESH,
        )

    @pl.loop(1, DEV)
    def _(k):
        a, b = to(k)
        take(b * NX_DEV + a)
        d_copy(k, (a, b), me_t).start()

    take(me_q)
    own = pltpu.make_async_copy(hsend.at[me_q], recv.at[me_t], lsem)
    own.start()

    own.wait()

    @pl.loop(1, DEV)
    def _(k):
        a, b = back(k)
        d_copy(k, (a, b), a * NY_DEV + b).wait()

    @pl.loop(0, DEV // 4)
    def _(i):
        recvf[pl.ds(pl.multiple_of(i * 128, 128), 128), :] = (
            recv[pl.ds(i * 4, 4)].reshape(128, 128).astype(F32)
        )

    @pl.loop(0, 8)
    def _(i):
        for j in range(2):

            @pl.loop(0, 8)
            def _(v):
                for u in range(16):
                    n = v * 16 + u
                    pulled[pl.ds(j * 128 + n, 1), :] = recvf[pl.ds(slot_s[i * 2 + j, n], 1), :]

        rows = pl.ds(pl.multiple_of(i * 256, 256), 256)
        x = pulled[...].astype(BF16)
        kb = kb_ref[rows, :]
        zero = jnp.zeros_like(x)
        total = jnp.zeros((256, 128), F32)
        for k in range(KINDS):
            masked = jnp.where(kb == jnp.asarray(k, BF16), x, zero)
            total = total + lax.dot_general(masked, spread_ref[k], NT, preferred_element_type=F32)
        grad_ref[rows, :] = deriv_ref[rows, :] * total


def local(cot_field, conductance, diagonal, source_adjoint, spreading, heat_deriv, block_tile, block_patch, block_kind):
    grid16 = (OWNED // 128, 128)
    shape = jax.ShapeDtypeStruct
    send, meta, slots, kinds = pl.pallas_call(
        route_kernel,
        out_shape=(
            shape((SLOTS, 128), BF16),
            shape((DEV, 128), I32),
            shape(grid16, I32),
            shape((OWNED, 128), BF16),
        ),
        in_specs=[VMEM] * 2,
        out_specs=(VMEM,) * 4,
        scratch_shapes=[
            pltpu.VMEM((OWNED, 128), F32),
            pltpu.VMEM((SLOTS, 128), F32),
            pltpu.SMEM(grid16, I32),
            pltpu.SemaphoreType.DMA,
        ],
        compiler_params=pltpu.CompilerParams(vmem_limit_bytes=20 << 20),
        name="route",
    )(
        jnp.concatenate([x.reshape(grid16) for x in (block_tile, block_patch, block_kind)]),
        source_adjoint,
    )

    dma = pltpu.SemaphoreType.DMA
    seeds, idx, got = pl.pallas_call(
        forward_kernel,
        out_shape=(shape((SLOTS, 128), F32), shape((DEV, 128), I32), shape((DEV, 128), I32)),
        in_specs=[VMEM] * 3,
        out_specs=(VMEM,) * 3,
        scratch_shapes=[
            pltpu.VMEM((DEV, CAP, 128), BF16),
            pltpu.VMEM((NX_DEV, NY_DEV, 128), I32),
            pltpu.VMEM((NY_DEV, NX_DEV, 128), I32),
            pltpu.VMEM((NY_DEV, NX_DEV, 128), I32),
            pltpu.VMEM((CAP, DEV), F32),
            dma((DEV,)),
            dma((DEV,)),
            dma((NX_DEV,)),
            dma((NX_DEV,)),
            dma((NY_DEV,)),
            dma((NY_DEV,)),
            dma((3,)),
        ],
        compiler_params=pltpu.CompilerParams(
            collective_id=0, has_side_effects=True, vmem_limit_bytes=24 << 20
        ),
        name="forward",
    )(
        send.reshape(DEV, CAP, 128),
        meta.reshape(NX_DEV, NY_DEV, 128),
        spreading.reshape(KINDS * 128, 128),
    )

    rhs = pl.pallas_call(
        scatter_kernel,
        out_shape=shape((ROWS, 128), F32),
        in_specs=[SMEM, SMEM, VMEM, ANY],
        out_specs=VMEM,
        scratch_shapes=[dma((CH * NZ,))],
        compiler_params=pltpu.CompilerParams(vmem_limit_bytes=24 << 20),
        name="scatter",
    )(idx, got, seeds, cot_field)

    flat = pltpu.VMEM((PATCHES, 128), F32)
    padded = pltpu.VMEM((GROWS, 128), F32)
    temp, grad = pl.pallas_call(
        backward_kernel,
        out_shape=(shape(cot_field.shape, F32), shape((OWNED, 128), F32)),
        in_specs=[SMEM, SMEM, VMEM, VMEM, VMEM, VMEM, VMEM, VMEM],
        out_specs=(VMEM, VMEM),
        scratch_shapes=[
            flat,
            padded,
            padded,
            pltpu.VMEM((ROWS, 128), F32),
            pltpu.VMEM((CAP, 128), F32),
            pltpu.VMEM((DEV, CAP, 128), BF16),
            pltpu.VMEM((DEV, CAP, 128), BF16),
            pltpu.VMEM((SLOTS, 128), F32),
            pltpu.VMEM((256, 128), F32),
            pltpu.VMEM((2, 2, CH * NZ, 128), F32),
            pltpu.VMEM((2, 2, 16, 128), F32),
            pltpu.VMEM((2, 2, CH * NZ, 128), F32),
            pltpu.VMEM((2, 2, 16, 128), F32),
            dma((DEV,)),
            dma((DEV,)),
            dma((2, 4)),
            dma((2, 4)),
            dma,
        ],
        compiler_params=pltpu.CompilerParams(
            collective_id=1, has_side_effects=True, vmem_limit_bytes=28 << 20
        ),
        name="backward",
    )(idx, slots, rhs, conductance, diagonal, kinds, spreading, heat_deriv)
    return temp, grad


def solution(mesh):
    blocks = P(("tx", "ty"))
    field = P(None, "tx", "ty")
    in_specs = (
        field, field, field, P(("tx", "ty"), None), P(), P(("tx", "ty"), None),
        P(("tx", "ty"), None), blocks, blocks,
    )
    out_specs = (field, P(("tx", "ty"), None))
    return jax.shard_map(local, mesh=mesh, in_specs=in_specs, out_specs=out_specs, check_vma=False)
```

```python
import functools

import jax
import jax.numpy as jnp
from jax import lax
from jax.experimental import pallas as pl
from jax.experimental.pallas import tpu as pltpu
from jax.sharding import PartitionSpec as P

NX_DEV, NY_DEV = 8, 16
DEV = NX_DEV * NY_DEV
CAP = 32
SLOTS = DEV * CAP
KINDS = 16
NZ, CX, CY = 8, 256, 512
CH = CY // 128
PATCHES = NZ * CX * CH
ROWS = PATCHES + CAP
SEG = CX + 16
GROWS = CH * (NZ + 2) * SEG
OWNED = 2048
GROUP = 8
AHEAD = 6
UNROLL, BATCH = 16, 1
F32, BF16, I32 = jnp.float32, jnp.bfloat16, jnp.int32
MESH = pl.DeviceIdType.MESH
VMEM = pl.BlockSpec(memory_space=pltpu.VMEM)
SMEM = pl.BlockSpec(memory_space=pltpu.SMEM)
ANY = pl.BlockSpec(memory_space=pl.ANY)
NT = (((1,), (1,)), ((), ()))


def dot(a, b):
    return jnp.dot(a, b, preferred_element_type=F32)


def iota(shape, dim):
    return lax.broadcasted_iota(I32, shape, dim)


def route(table_ref, slot_ref, kb_ref):
    sub, lane = iota((128, 128), 0), iota((128, 128), 1)
    before = (sub < lane).astype(F32).astype(BF16)
    ones = jnp.ones((128, 128), BF16)
    rank_row = iota((CAP, 128), 0)
    count = jnp.zeros((128, 128), F32)
    held = jnp.zeros((128, 128), F32)
    block = jnp.zeros((CAP, 128), F32)
    for j in range(OWNED // 128):
        tile, patch, kind = (table_ref[n * 16 + j : n * 16 + j + 1, :] for n in range(3))
        place = (patch & (CH - 1)) * (NZ * CX) + (patch >> 2)
        hit = (sub == tile).astype(F32)
        hit16 = hit.astype(BF16)
        rank = jnp.sum(hit * (dot(hit16, before) + count), axis=0, keepdims=True).astype(I32)
        count = count + dot(hit16, ones)
        slot_ref[j : j + 1, :] = tile * CAP + rank
        at = (rank_row == rank).astype(F32)
        parts = jnp.concatenate(
            [
                at * (place >> 7).astype(F32),
                at * (place & 127).astype(F32),
                at * (kind + 1).astype(F32),
                jnp.zeros((128 - 3 * CAP, 128), F32),
            ],
            axis=0,
        ).astype(BF16)
        held = held + lax.dot_general(hit16, parts, NT, preferred_element_type=F32)
        numbers = jnp.concatenate([at * iota((1, 128), 1).astype(F32), at], axis=0).astype(BF16)
        found = lax.dot_general(numbers, hit16, NT, preferred_element_type=F32)
        block = block + found[:CAP] + found[CAP:] * (128.0 * j)
        kb_ref[pl.ds(j * 128, 128), :] = jnp.transpose(
            jnp.broadcast_to(kind.astype(F32), (128, 128))
        ).astype(BF16)
    counts = count.astype(I32)
    place = (held * 128.0 + pltpu.roll(held, 128 - CAP, 1)).astype(I32)
    kind1 = pltpu.roll(held, 128 - 2 * CAP, 1).astype(I32)
    place = jnp.where(lane < counts, place, PATCHES + lane)
    within = lane & (GROUP - 1)
    clash = jnp.zeros((128, 128), I32)
    for k in range(1, GROUP):
        same = (pltpu.roll(place, k, 1) == place) & (within >= k)
        clash = jnp.maximum(clash, same.astype(I32))
    for k in (1, 2, 4, 8):
        if k < GROUP:
            clash = jnp.maximum(clash, jnp.where(within >= k, pltpu.roll(clash, k, 1), 0))
    meta = place + kind1 * 16384 + clash * (1 << 20)
    return jnp.where(lane < CAP, meta, counts), block.astype(I32) & (OWNED - 1)


def partners():
    tx, ty = lax.axis_index("tx"), lax.axis_index("ty")

    def to(g, i):
        return lax.rem(tx + i, NX_DEV), lax.rem(ty + g * 5, NY_DEV)

    def from_y(g):
        return lax.rem(ty + 5 * NY_DEV - g * 5, NY_DEV)

    return tx, ty, to, from_y


def each(do, lo=0, hi=NY_DEV):
    if lo == 0:
        for i in range(1, NX_DEV):
            do(0, i)

    @pl.loop(max(lo, 1), hi)
    def _(g):
        for i in range(NX_DEV):
            do(g, i)


def greet_all(to):
    barrier = pltpu.get_barrier_semaphore()
    each(
        lambda g, i: pl.semaphore_signal(barrier, inc=1, device_id=to(g, i), device_id_type=MESH)
    )
    return barrier


def wait_for(src, dst, n, at, send_sem, recv_sem, peer):
    return pltpu.make_async_remote_copy(
        src_ref=src.at[pl.ds(at, n)], dst_ref=dst.at[pl.ds(at, n)],
        send_sem=send_sem, recv_sem=recv_sem, device_id=peer, device_id_type=MESH,
    )


def forward_kernel(
    table_ref, src_ref, spread_ref,
    seed_ref, idx_ref, meta_ref, slot_ref, kb_ref,
    srcf, rows_f, send, mine, block_v, block_s, recv, mid, mid2, last, kcol,
    ssem, rsem, xs, xr, ys, yr, lsem,
):
    tx, ty, to, from_y = partners()
    me_t, me_q = tx * NY_DEV + ty, ty * NX_DEV + tx
    barrier = greet_all(to)
    meta, block = route(table_ref, slot_ref, kb_ref)
    block_v[...] = block
    fetch = pltpu.make_async_copy(block_v, block_s, lsem.at[3])
    fetch.start()
    for i in range(NX_DEV):
        mine[i] = meta[i * NY_DEV : (i + 1) * NY_DEV, :]
    own_mid = pltpu.make_async_copy(mine.at[tx], mid.at[tx], lsem.at[1])
    own_mid.start()

    @pl.loop(0, OWNED // 128)
    def _(i):
        at = pl.ds(pl.multiple_of(i * 128, 128), 128)
        srcf[at, :] = src_ref[at, :].astype(F32)

    fetch.wait()
    pl.semaphore_wait(barrier, DEV - 1)

    def pack(t):
        for u in range(CAP):
            rows_f[u : u + 1, :] = srcf[pl.ds(block_s[u, t], 1), :]
        send[t] = rows_f[...].astype(BF16)

    def x_copy(i, peer, there):
        return pltpu.make_async_remote_copy(
            src_ref=mine.at[peer], dst_ref=mid.at[there], send_sem=xs.at[i],
            recv_sem=xr.at[i], device_id=(peer, ty), device_id_type=MESH,
        )

    def y_copy(i, peer, there):
        return pltpu.make_async_remote_copy(
            src_ref=mid2.at[peer], dst_ref=last.at[there], send_sem=ys.at[i],
            recv_sem=yr.at[i], device_id=(tx, peer), device_id_type=MESH,
        )


    @pl.loop(1, NX_DEV)
    def _(i):
        x_copy(i, (tx + i) % NX_DEV, tx).start()

    def post(g, i):
        a, b = to(g, i)
        t = a * NY_DEV + b
        pack(t)
        pltpu.make_async_remote_copy(
            src_ref=send.at[t], dst_ref=recv.at[me_q], send_sem=ssem,
            recv_sem=rsem.at[g], device_id=(a, b), device_id_type=MESH,
        ).start()

    each(post, 0, 2)
    own_mid.wait()

    @pl.loop(1, NX_DEV)
    def _(i):
        x_copy(i, (tx + NX_DEV - i) % NX_DEV, (tx + NX_DEV - i) % NX_DEV).wait()

    for j in range(NY_DEV):
        mid2[j] = mid[:, j, :]
    own_meta = pltpu.make_async_copy(mid2.at[ty], last.at[ty], lsem.at[2])
    own_meta.start()

    @pl.loop(1, NY_DEV)
    def _(i):
        y_copy(i, (ty + i) % NY_DEV, ty).start()

    each(post, 2, AHEAD)
    pack(me_t)
    own = pltpu.make_async_copy(send.at[me_t], recv.at[me_q], lsem.at[0])
    own.start()
    own_meta.wait()
    own.wait()

    @pl.loop(1, NY_DEV)
    def _(i):
        y_copy(i, (ty + NY_DEV - i) % NY_DEV, (ty + NY_DEV - i) % NY_DEV).wait()

    meta = last[...].reshape(DEV, 128)
    meta_ref[...] = meta
    idx_ref[...] = meta & 16383
    kind1 = jnp.transpose(((meta >> 14) & 31).astype(F32))[:CAP, :]
    kcol[...] = kind1

    @pl.loop(0, NY_DEV)
    def _(g):
        @pl.when(g < NY_DEV - AHEAD)
        def _():
            for i in range(NX_DEV):
                post(g + AHEAD, i)

        q = from_y(g)

        @pl.when(g == 0)
        def _():
            wait_for(send, recv, NX_DEV - 1, 0, ssem, rsem.at[0], to(0, 1)).wait_recv()

        @pl.when(g > 0)
        def _():
            wait_for(send, recv, NX_DEV, q * NX_DEV, ssem, rsem.at[g], to(0, 1)).wait_recv()

        kinds = pltpu.roll(kcol[...], (DEV - q * NX_DEV) % DEV, 1)
        kb = jnp.concatenate(
            [jnp.broadcast_to(kinds[:, i : i + 1], (CAP, 128)) for i in range(NX_DEV)], axis=0
        ).astype(BF16)
        x = recv[pl.ds(q * NX_DEV, NX_DEV)].reshape(NX_DEV * CAP, 128)
        zero = jnp.zeros_like(x)
        masked = jnp.concatenate(
            [jnp.where(kb == jnp.asarray(k + 1, BF16), x, zero) for k in range(KINDS)], axis=1
        )
        rows = pl.ds(pl.multiple_of(q * (NX_DEV * CAP), NX_DEV * CAP), NX_DEV * CAP)
        seed_ref[rows, :] = dot(masked, spread_ref[...])

    wait_for(send, recv, DEV - 1, 0, ssem, rsem.at[0], to(0, 1)).wait_send()


def scatter_kernel(idx_s, meta_s, seed_ref, *refs):
    fields, acc, held, sem = refs[:3], refs[3], refs[4:7], refs[7]
    loads = [pltpu.make_async_copy(f, h, sem.at[n]) for n, (f, h) in enumerate(zip(fields, held))]
    for load in loads:
        load.start()

    @pl.loop(0, ROWS // 32)
    def _(i):
        acc[pl.ds(pl.multiple_of(i * 32, 32), 32), :] = jnp.zeros((32, 128), F32)

    @pl.loop(0, DEV)
    def _(q):
        count = meta_s[q, CAP]
        for g in range(CAP // GROUP):

            @pl.when(count > g * GROUP)
            def _():
                base = pl.multiple_of(q * CAP + g * GROUP, GROUP)
                at = [pl.ds(idx_s[q, g * GROUP + u], 1) for u in range(GROUP)]
                clash = meta_s[q, g * GROUP + GROUP - 1]

                @pl.when(clash < (1 << 20))
                def _():
                    new = [acc[at[u], :] + seed_ref[pl.ds(base + u, 1), :] for u in range(GROUP)]
                    for u in range(GROUP):
                        acc[at[u], :] = new[u]

                @pl.when(clash >= (1 << 20))
                def _():
                    for u in range(GROUP):
                        acc[at[u], :] = acc[at[u], :] + seed_ref[pl.ds(base + u, 1), :]

    for load in loads:
        load.wait()


def backward_kernel(
    idx_s, cot_ref, cond_ref, diag_ref, add_ref,
    out_ref, recvf,
    rhs, inv, g0, g1, adj, heat, hsend, recv,
    xe, ye, xh, yh,
    ssem, rsem, hs, hr, lsem,
):
    tx, ty, to, from_y = partners()
    me_t, me_q = tx * NY_DEV + ty, ty * NX_DEV + tx
    lane = iota((8, 128), 1)
    barrier = greet_all(to)
    adj[pl.ds(PATCHES, CAP), :] = jnp.zeros((CAP, 128), F32)
    for g in (g0, g1):
        for c in range(CH):
            for l in (0, NZ + 1):

                @pl.loop(0, CX // 64)
                def _(i):
                    g[pl.ds((c * (NZ + 2) + l) * SEG + 8 + i * 64, 64), :] = jnp.zeros((64, 128), F32)

    def cell(c, l, r):
        return l, pl.ds(r, 8), pl.ds(c * 128, 128)

    def row_of(c, l, r):
        return pl.ds(pl.multiple_of(c * (NZ * CX) + l * CX + r, 8), 8)

    def grow_of(c, l, r):
        return pl.multiple_of((c * (NZ + 2) + l + 1) * SEG + 8 + r, 8)

    def edges(acc, lo, hi, j):
        left, right = acc
        left = jnp.where(lane == j, pltpu.roll(lo, j, 1), left)
        right = jnp.where(lane == j, pltpu.roll(hi, (j + 1) % 128, 1), right)
        return left, right

    def visit(body, after=None):
        for h in range(2):

            def step(i, acc):
                for v in range(0, UNROLL, BATCH):
                    stores = []
                    for u in range(v, v + BATCH):
                        j = i * UNROLL + u
                        r = pl.multiple_of((i % (32 // UNROLL)) * (UNROLL * 8), 8) + u * 8
                        writes, lo, hi = body(h * 4 + i // (32 // UNROLL), r, j, h)
                        stores += writes
                        if after is not None:
                            acc = edges(acc, lo, hi, j)
                    for ref, at, value in stores:
                        ref[at] = value
                return acc

            acc = lax.fori_loop(0, 128 // UNROLL, step, (jnp.zeros((8, 128), F32),) * 2)
            if after is not None:
                after(h, acc)

    def keep_edges(s):
        def after(h, acc):
            ye[s, 0, pl.ds(h * 8, 8), :] = acc[0]
            ye[s, 1, pl.ds(h * 8, 8), :] = acc[1]

        return after

    def start(l, r, j, h):
        writes, ends = [], []
        for c in range(CH):
            at = row_of(c, l, r), slice(None)
            q = 1.0 / diag_ref[cell(c, l, r)]
            value = cot_ref[cell(c, l, r)] + add_ref[at]
            g = cond_ref[cell(c, l, r)] * (value * q)
            writes.append((rhs, at, value))
            writes.append((inv, at, q))
            writes.append((g0, (pl.ds(grow_of(c, l, r), 8), slice(None)), g))
            ends.append(g)
        return writes, ends[0], ends[-1]

    def sums(g, s, l, r, j, h):
        own = [g[pl.ds(grow_of(c, l, r), 8), :] for c in range(CH)]
        before = pltpu.roll(yh[s, 0, pl.ds(h * 8, 8), :], 127 - j, 1)
        behind = pltpu.roll(yh[s, 1, pl.ds(h * 8, 8), :], (128 - j) % 128, 1)
        wide = [before, *own, behind]
        out = []
        for c in range(CH):
            b = grow_of(c, l, r)
            west = pltpu.roll(jnp.where(lane == 127, wide[c], own[c]), 1, 1)
            east = pltpu.roll(jnp.where(lane == 0, wide[c + 2], own[c]), 127, 1)
            total = g[pl.ds(b - 1, 8), :] + g[pl.ds(b + 1, 8), :]
            total = total + west + east
            out.append(total + g[pl.ds(b - SEG, 8), :] + g[pl.ds(b + SEG, 8), :])
        return out

    def first(l, r, j, h):
        writes, ends = [], []
        for c, total in enumerate(sums(g0, 0, l, r, j, h)):
            at = row_of(c, l, r), slice(None)
            g = cond_ref[cell(c, l, r)] * ((rhs[at] + total) * inv[at])
            writes.append((g1, (pl.ds(grow_of(c, l, r), 8), slice(None)), g))
            ends.append(g)
        return writes, ends[0], ends[-1]

    def second(l, r, j, h):
        writes = []
        for c, total in enumerate(sums(g1, 1, l, r, j, h)):
            at = row_of(c, l, r), slice(None)
            value = (rhs[at] + total) * inv[at]
            writes.append((adj, at, value))
            writes.append((out_ref, cell(c, l, r), value))
        return writes, None, None

    up, down = (tx + NX_DEV - 1) % NX_DEV, (tx + 1) % NX_DEV
    west, east = (ty + NY_DEV - 1) % NY_DEV, (ty + 1) % NY_DEV

    def halo(s, g):
        for c in range(CH):
            for l in range(NZ):
                n = c * NZ + l
                b = (c * (NZ + 2) + l + 1) * SEG + 8
                xe[s, 0, n : n + 1, :] = g[b : b + 1, :]
                xe[s, 1, n : n + 1, :] = g[b + CX - 1 : b + CX, :]
        if s == 0:
            pl.semaphore_wait(barrier, DEV - 1)
        copies = []
        for i, (src, dst, dev) in enumerate(
            (
                (ye.at[s, 0], yh.at[s, 1], (tx, west)),
                (ye.at[s, 1], yh.at[s, 0], (tx, east)),
                (xe.at[s, 0], xh.at[s, 1], (up, ty)),
                (xe.at[s, 1], xh.at[s, 0], (down, ty)),
            )
        ):
            copies.append(
                pltpu.make_async_remote_copy(
                    src_ref=src, dst_ref=dst, send_sem=hs.at[s, i], recv_sem=hr.at[s, i],
                    device_id=dev, device_id_type=MESH,
                )
            )
            copies[-1].start()
        for copy in copies:
            copy.wait()
        outer = jnp.where(tx == 0, 0.0, xh[s, 0])
        outer2 = jnp.where(tx == NX_DEV - 1, 0.0, xh[s, 1])
        for c in range(CH):
            for l in range(NZ):
                n = c * NZ + l
                b = (c * (NZ + 2) + l + 1) * SEG + 8
                g[b - 1 : b, :] = outer[n : n + 1, :]
                g[b + CX : b + CX + 1, :] = outer2[n : n + 1, :]
        yh[s, 0] = jnp.where(ty == 0, 0.0, yh[s, 0])
        yh[s, 1] = jnp.where(ty == NY_DEV - 1, 0.0, yh[s, 1])

    visit(start, keep_edges(0))
    halo(0, g0)
    visit(first, keep_edges(1))
    halo(1, g1)
    visit(second)

    def take(q):
        for u in range(CAP):
            heat[pl.ds(u, 1), :] = adj[pl.ds(idx_s[q, u], 1), :]
        hsend[q] = heat[...].astype(BF16)

    def post(g, i):
        a, b = to(g, i)
        q = b * NX_DEV + a
        take(q)
        pltpu.make_async_remote_copy(
            src_ref=hsend.at[q], dst_ref=recv.at[me_t], send_sem=ssem,
            recv_sem=rsem, device_id=(a, b), device_id_type=MESH,
        ).start()

    each(post)
    take(me_q)
    own = pltpu.make_async_copy(hsend.at[me_q], recv.at[me_t], lsem)
    own.start()

    own.wait()

    wait_for(hsend, recv, DEV - 1, 0, ssem, rsem, to(0, 1)).wait()

    @pl.loop(0, DEV // 4)
    def _(i):
        recvf[pl.ds(pl.multiple_of(i * 128, 128), 128), :] = (
            recv[pl.ds(i * 4, 4)].reshape(128, 128).astype(F32)
        )


def pull_kernel(slot_s, recvf, kb_ref, spread_ref, deriv_ref, temp_ref, out_ref, grad_ref, even, odd, sem):
    save = pltpu.make_async_copy(temp_ref, out_ref, sem)
    save.start()

    def gather(i, rows):
        for n in range(256):
            rows[n : n + 1, :] = recvf[pl.ds(slot_s[i * 2 + n // 128, n % 128], 1), :]

    def pull(i, rows):
        at = pl.ds(pl.multiple_of(i * 256, 256), 256)
        x = rows[...].astype(BF16)
        kb = kb_ref[at, :]
        zero = jnp.zeros_like(x)
        masked = jnp.concatenate(
            [jnp.where(kb == jnp.asarray(k, BF16), x, zero) for k in range(KINDS)], axis=1
        )
        wide = jnp.concatenate([spread_ref[k] for k in range(KINDS)], axis=1)
        total = lax.dot_general(masked, wide, NT, preferred_element_type=F32)
        grad_ref[at, :] = deriv_ref[at, :] * total

    gather(0, even)

    @pl.loop(0, 4)
    def _(i):
        gather(2 * i + 1, odd)
        pull(2 * i, even)
        gather(jnp.minimum(2 * i + 2, 7), even)
        pull(2 * i + 1, odd)

    save.wait()


def local(cot_field, conductance, diagonal, source_adjoint, spreading, heat_deriv, block_tile, block_patch, block_kind):
    grid16 = (OWNED // 128, 128)
    shape = jax.ShapeDtypeStruct
    dma = pltpu.SemaphoreType.DMA
    seeds, idx, got, slots, kinds = pl.pallas_call(
        forward_kernel,
        out_shape=(
            shape((SLOTS, 128), F32),
            shape((DEV, 128), I32),
            shape((DEV, 128), I32),
            shape(grid16, I32),
            shape((OWNED, 128), BF16),
        ),
        in_specs=[VMEM] * 3,
        out_specs=(VMEM,) * 5,
        scratch_shapes=[
            pltpu.VMEM((OWNED, 128), F32),
            pltpu.VMEM((CAP, 128), F32),
            pltpu.VMEM((DEV, CAP, 128), BF16),
            pltpu.VMEM((NX_DEV, NY_DEV, 128), I32),
            pltpu.VMEM((CAP, DEV), I32),
            pltpu.SMEM((CAP, DEV), I32),
            pltpu.VMEM((DEV, CAP, 128), BF16),
            pltpu.VMEM((NX_DEV, NY_DEV, 128), I32),
            pltpu.VMEM((NY_DEV, NX_DEV, 128), I32),
            pltpu.VMEM((NY_DEV, NX_DEV, 128), I32),
            pltpu.VMEM((CAP, DEV), F32),
            dma,
            dma((NY_DEV,)),
            dma((NX_DEV,)),
            dma((NX_DEV,)),
            dma((NY_DEV,)),
            dma((NY_DEV,)),
            dma((4,)),
        ],
        compiler_params=pltpu.CompilerParams(
            collective_id=0, has_side_effects=True, vmem_limit_bytes=12 << 20
        ),
        name="forward",
    )(
        jnp.concatenate([x.reshape(grid16) for x in (block_tile, block_patch, block_kind)]),
        source_adjoint,
        spreading.reshape(KINDS * 128, 128),
    )

    hbm = pl.BlockSpec(memory_space=pltpu.MemorySpace.HBM)
    added, *fields = pl.pallas_call(
        scatter_kernel,
        out_shape=(shape((ROWS, 128), F32),) + (shape(cot_field.shape, F32),) * 3,
        in_specs=[SMEM, SMEM, VMEM] + [hbm] * 3,
        out_specs=(VMEM,) * 4,
        scratch_shapes=[dma((3,))],
        compiler_params=pltpu.CompilerParams(vmem_limit_bytes=36 << 20),
        name="scatter",
    )(idx, got, seeds, cot_field, conductance, diagonal)

    flat = pltpu.VMEM((PATCHES, 128), F32)
    padded = pltpu.VMEM((GROWS, 128), F32)
    temp, heat = pl.pallas_call(
        backward_kernel,
        out_shape=(shape(cot_field.shape, F32), shape((SLOTS, 128), F32)),
        in_specs=[SMEM] + [VMEM] * 4,
        out_specs=(VMEM, VMEM),
        scratch_shapes=[
            flat,
            flat,
            padded,
            padded,
            pltpu.VMEM((ROWS, 128), F32),
            pltpu.VMEM((CAP, 128), F32),
            pltpu.VMEM((DEV, CAP, 128), BF16),
            pltpu.VMEM((DEV, CAP, 128), BF16),
            pltpu.VMEM((2, 2, CH * NZ, 128), F32),
            pltpu.VMEM((2, 2, 16, 128), F32),
            pltpu.VMEM((2, 2, CH * NZ, 128), F32),
            pltpu.VMEM((2, 2, 16, 128), F32),
            dma,
            dma,
            dma((2, 4)),
            dma((2, 4)),
            dma,
        ],
        compiler_params=pltpu.CompilerParams(
            collective_id=1, has_side_effects=True, vmem_limit_bytes=30 << 20
        ),
        name="backward",
    )(idx, *fields, added)

    return pl.pallas_call(
        pull_kernel,
        out_shape=(shape(cot_field.shape, F32), shape((OWNED, 128), F32)),
        in_specs=[SMEM, VMEM, VMEM, VMEM, VMEM, VMEM],
        out_specs=(ANY, VMEM),
        scratch_shapes=[pltpu.VMEM((256, 128), F32), pltpu.VMEM((256, 128), F32), dma],
        compiler_params=pltpu.CompilerParams(vmem_limit_bytes=16 << 20),
        name="pull",
    )(slots, heat, kinds, spreading, heat_deriv, temp)


def solution(mesh):
    blocks = P(("tx", "ty"))
    field = P(None, "tx", "ty")
    in_specs = (
        field, field, field, P(("tx", "ty"), None), P(), P(("tx", "ty"), None),
        P(("tx", "ty"), None), blocks, blocks,
    )
    out_specs = (field, P(("tx", "ty"), None))
    return jax.shard_map(local, mesh=mesh, in_specs=in_specs, out_specs=out_specs, check_vma=False)
```

```python
import functools

import jax
import jax.numpy as jnp
from jax import lax
from jax.experimental import pallas as pl
from jax.experimental.pallas import tpu as pltpu
from jax.sharding import PartitionSpec as P

NX_DEV, NY_DEV = 8, 16
DEV = NX_DEV * NY_DEV
CAP = 32
SLOTS = DEV * CAP
KINDS = 16
NZ, CX, CY = 8, 256, 512
CH = CY // 128
PATCHES = NZ * CX * CH
ROWS = PATCHES + CAP
SEG = CX + 16
GROWS = CH * (NZ + 2) * SEG
OWNED = 2048
GROUP = 8
CLASH = 8
AHEAD = 6
UNROLL, BATCH = 16, 1
F32, BF16, I32 = jnp.float32, jnp.bfloat16, jnp.int32
MESH = pl.DeviceIdType.MESH
VMEM = pl.BlockSpec(memory_space=pltpu.VMEM)
SMEM = pl.BlockSpec(memory_space=pltpu.SMEM)
ANY = pl.BlockSpec(memory_space=pl.ANY)
NT = (((1,), (1,)), ((), ()))


def dot(a, b):
    return jnp.dot(a, b, preferred_element_type=F32)


def iota(shape, dim):
    return lax.broadcasted_iota(I32, shape, dim)


def route(table_ref, slot_ref, kb_ref):
    sub, lane = iota((128, 128), 0), iota((128, 128), 1)
    before = (sub < lane).astype(F32).astype(BF16)
    ones = jnp.ones((128, 128), BF16)
    rank_row = iota((CAP, 128), 0)
    count = jnp.zeros((128, 128), F32)
    held = jnp.zeros((128, 128), F32)
    block = jnp.zeros((CAP, 128), F32)
    for j in range(OWNED // 128):
        tile, patch, kind = (table_ref[n * 16 + j : n * 16 + j + 1, :] for n in range(3))
        place = (patch & (CH - 1)) * (NZ * CX) + (patch >> 2)
        hit = (sub == tile).astype(F32)
        hit16 = hit.astype(BF16)
        rank = jnp.sum(hit * (dot(hit16, before) + count), axis=0, keepdims=True).astype(I32)
        count = count + dot(hit16, ones)
        slot_ref[j : j + 1, :] = tile * CAP + rank
        at = (rank_row == rank).astype(F32)
        parts = jnp.concatenate(
            [
                at * (place >> 7).astype(F32),
                at * (place & 127).astype(F32),
                at * (kind + 1).astype(F32),
                jnp.zeros((128 - 3 * CAP, 128), F32),
            ],
            axis=0,
        ).astype(BF16)
        held = held + lax.dot_general(hit16, parts, NT, preferred_element_type=F32)
        numbers = jnp.concatenate([at * iota((1, 128), 1).astype(F32), at], axis=0).astype(BF16)
        found = lax.dot_general(numbers, hit16, NT, preferred_element_type=F32)
        block = block + found[:CAP] + found[CAP:] * (128.0 * j)
        kb_ref[pl.ds(j * 128, 128), :] = jnp.transpose(
            jnp.broadcast_to(kind.astype(F32), (128, 128))
        ).astype(BF16)
    counts = count.astype(I32)
    place = (held * 128.0 + pltpu.roll(held, 128 - CAP, 1)).astype(I32)
    kind1 = pltpu.roll(held, 128 - 2 * CAP, 1).astype(I32)
    place = jnp.where(lane < counts, place, PATCHES + lane)
    clash = jnp.zeros((128, 128), I32)
    for k in range(1, CAP):
        same = (pltpu.roll(place, k, 1) == place) & (lane >= k) & (lane < counts)
        clash = jnp.maximum(clash, same.astype(I32))
    clash = jnp.max(clash, axis=1, keepdims=True)
    groups = (counts + (GROUP - 1)) // GROUP + clash * CLASH
    return jnp.where(lane < CAP, place + kind1 * 16384, groups), block.astype(I32) & (OWNED - 1)


def partners():
    tx, ty = lax.axis_index("tx"), lax.axis_index("ty")

    def to(g, i):
        return lax.rem(tx + i, NX_DEV), lax.rem(ty + g * 5, NY_DEV)

    def from_y(g):
        return lax.rem(ty + 5 * NY_DEV - g * 5, NY_DEV)

    return tx, ty, to, from_y


def each(do, lo=0, hi=NY_DEV):
    if lo == 0:
        for i in range(1, NX_DEV):
            do(0, i)

    @pl.loop(max(lo, 1), hi)
    def _(g):
        for i in range(NX_DEV):
            do(g, i)


def greet_all(to):
    barrier = pltpu.get_barrier_semaphore()
    each(
        lambda g, i: pl.semaphore_signal(barrier, inc=1, device_id=to(g, i), device_id_type=MESH)
    )
    return barrier


def wait_for(src, dst, n, at, send_sem, recv_sem, peer):
    return pltpu.make_async_remote_copy(
        src_ref=src.at[pl.ds(at, n)], dst_ref=dst.at[pl.ds(at, n)],
        send_sem=send_sem, recv_sem=recv_sem, device_id=peer, device_id_type=MESH,
    )


def forward_kernel(
    table_ref, src_ref, spread_ref,
    seed_ref, idx_ref, meta_ref, slot_ref, kb_ref,
    srcf, rows_f, send, mine, block_v, block_s, recv, mid, mid2, last, kcol,
    ssem, rsem, xs, xr, ys, yr, lsem,
):
    tx, ty, to, from_y = partners()
    me_t, me_q = tx * NY_DEV + ty, ty * NX_DEV + tx
    barrier = greet_all(to)
    meta, block = route(table_ref, slot_ref, kb_ref)
    block_v[...] = block
    fetch = pltpu.make_async_copy(block_v, block_s, lsem.at[3])
    fetch.start()
    for i in range(NX_DEV):
        mine[i] = meta[i * NY_DEV : (i + 1) * NY_DEV, :]
    own_mid = pltpu.make_async_copy(mine.at[tx], mid.at[tx], lsem.at[1])
    own_mid.start()

    @pl.loop(0, OWNED // 128)
    def _(i):
        at = pl.ds(pl.multiple_of(i * 128, 128), 128)
        srcf[at, :] = src_ref[at, :].astype(F32)

    fetch.wait()
    pl.semaphore_wait(barrier, DEV - 1)

    def pack(t):
        for u in range(CAP):
            rows_f[u : u + 1, :] = srcf[pl.ds(block_s[u, t], 1), :]
        send[t] = rows_f[...].astype(BF16)

    def x_copy(i, peer, there):
        return pltpu.make_async_remote_copy(
            src_ref=mine.at[peer], dst_ref=mid.at[there], send_sem=xs.at[i],
            recv_sem=xr.at[i], device_id=(peer, ty), device_id_type=MESH,
        )

    def y_copy(i, peer, there):
        return pltpu.make_async_remote_copy(
            src_ref=mid2.at[peer], dst_ref=last.at[there], send_sem=ys.at[i],
            recv_sem=yr.at[i], device_id=(tx, peer), device_id_type=MESH,
        )


    @pl.loop(1, NX_DEV)
    def _(i):
        x_copy(i, (tx + i) % NX_DEV, tx).start()

    def post(g, i):
        a, b = to(g, i)
        t = a * NY_DEV + b
        pack(t)
        pltpu.make_async_remote_copy(
            src_ref=send.at[t], dst_ref=recv.at[me_q], send_sem=ssem,
            recv_sem=rsem.at[g], device_id=(a, b), device_id_type=MESH,
        ).start()

    each(post, 0, 2)
    own_mid.wait()

    @pl.loop(1, NX_DEV)
    def _(i):
        x_copy(i, (tx + NX_DEV - i) % NX_DEV, (tx + NX_DEV - i) % NX_DEV).wait()

    for j in range(NY_DEV):
        mid2[j] = mid[:, j, :]
    own_meta = pltpu.make_async_copy(mid2.at[ty], last.at[ty], lsem.at[2])
    own_meta.start()

    @pl.loop(1, NY_DEV)
    def _(i):
        y_copy(i, (ty + i) % NY_DEV, ty).start()

    each(post, 2, AHEAD)
    pack(me_t)
    own = pltpu.make_async_copy(send.at[me_t], recv.at[me_q], lsem.at[0])
    own.start()
    own_meta.wait()
    own.wait()

    @pl.loop(1, NY_DEV)
    def _(i):
        y_copy(i, (ty + NY_DEV - i) % NY_DEV, (ty + NY_DEV - i) % NY_DEV).wait()

    meta = last[...].reshape(DEV, 128)
    meta_ref[...] = meta
    idx_ref[...] = meta & 16383
    kind1 = jnp.transpose(((meta >> 14) & 31).astype(F32))[:CAP, :]
    kcol[...] = kind1

    @pl.loop(0, NY_DEV)
    def _(g):
        @pl.when(g < NY_DEV - AHEAD)
        def _():
            for i in range(NX_DEV):
                post(g + AHEAD, i)

        q = from_y(g)

        @pl.when(g == 0)
        def _():
            wait_for(send, recv, NX_DEV - 1, 0, ssem, rsem.at[0], to(0, 1)).wait_recv()

        @pl.when(g > 0)
        def _():
            wait_for(send, recv, NX_DEV, q * NX_DEV, ssem, rsem.at[g], to(0, 1)).wait_recv()

        kinds = pltpu.roll(kcol[...], (DEV - q * NX_DEV) % DEV, 1)
        kb = jnp.concatenate(
            [jnp.broadcast_to(kinds[:, i : i + 1], (CAP, 128)) for i in range(NX_DEV)], axis=0
        ).astype(BF16)
        x = recv[pl.ds(q * NX_DEV, NX_DEV)].reshape(NX_DEV * CAP, 128)
        zero = jnp.zeros_like(x)
        masked = jnp.concatenate(
            [jnp.where(kb == jnp.asarray(k + 1, BF16), x, zero) for k in range(KINDS)], axis=1
        )
        rows = pl.ds(pl.multiple_of(q * (NX_DEV * CAP), NX_DEV * CAP), NX_DEV * CAP)
        seed_ref[rows, :] = dot(masked, spread_ref[...])

    wait_for(send, recv, DEV - 1, 0, ssem, rsem.at[0], to(0, 1)).wait_send()


def scatter_kernel(idx_s, meta_s, seed_ref, *refs):
    fields, acc, held, sem = refs[:3], refs[3], refs[4:7], refs[7]
    loads = [pltpu.make_async_copy(f, h, sem.at[n]) for n, (f, h) in enumerate(zip(fields, held))]
    for load in loads:
        load.start()

    @pl.loop(0, ROWS // 32)
    def _(i):
        acc[pl.ds(pl.multiple_of(i * 32, 32), 32), :] = jnp.zeros((32, 128), F32)

    @pl.loop(0, DEV)
    def _(q):
        groups = meta_s[q, CAP]
        base = pl.multiple_of(q * CAP, CAP)
        for n in range(1, CAP // GROUP + 1):

            @pl.when(groups == n)
            def _():
                at = [pl.ds(idx_s[q, u], 1) for u in range(n * GROUP)]
                new = [acc[at[u], :] + seed_ref[pl.ds(base + u, 1), :] for u in range(n * GROUP)]
                for u in range(n * GROUP):
                    acc[at[u], :] = new[u]

        @pl.when(groups > CLASH)
        def _():
            for u in range(CAP):
                at = pl.ds(idx_s[q, u], 1)
                acc[at, :] = acc[at, :] + seed_ref[pl.ds(base + u, 1), :]

    for load in loads:
        load.wait()


def backward_kernel(
    idx_s, cot_ref, cond_ref, diag_ref, add_ref,
    out_ref, recvf,
    rhs, inv, g0, g1, adj, heat, hsend, recv,
    xe, ye, xh, yh,
    ssem, rsem, hs, hr, lsem,
):
    tx, ty, to, from_y = partners()
    me_t, me_q = tx * NY_DEV + ty, ty * NX_DEV + tx
    lane = iota((8, 128), 1)
    barrier = greet_all(to)
    adj[pl.ds(PATCHES, CAP), :] = jnp.zeros((CAP, 128), F32)
    for g in (g0, g1):
        for c in range(CH):
            for l in (0, NZ + 1):

                @pl.loop(0, CX // 64)
                def _(i):
                    g[pl.ds((c * (NZ + 2) + l) * SEG + 8 + i * 64, 64), :] = jnp.zeros((64, 128), F32)

    def cell(c, l, r):
        return l, pl.ds(r, 8), pl.ds(c * 128, 128)

    def row_of(c, l, r):
        return pl.ds(pl.multiple_of(c * (NZ * CX) + l * CX + r, 8), 8)

    def grow_of(c, l, r):
        return pl.multiple_of((c * (NZ + 2) + l + 1) * SEG + 8 + r, 8)

    def edges(acc, lo, hi, j):
        left, right = acc
        left = jnp.where(lane == j, pltpu.roll(lo, j, 1), left)
        right = jnp.where(lane == j, pltpu.roll(hi, (j + 1) % 128, 1), right)
        return left, right

    def visit(body, after=None):
        for h in range(2):

            def step(i, acc):
                for v in range(0, UNROLL, BATCH):
                    stores = []
                    for u in range(v, v + BATCH):
                        j = i * UNROLL + u
                        r = pl.multiple_of((i % (32 // UNROLL)) * (UNROLL * 8), 8) + u * 8
                        writes, lo, hi = body(h * 4 + i // (32 // UNROLL), r, j, h)
                        stores += writes
                        if after is not None:
                            acc = edges(acc, lo, hi, j)
                    for ref, at, value in stores:
                        ref[at] = value
                return acc

            acc = lax.fori_loop(0, 128 // UNROLL, step, (jnp.zeros((8, 128), F32),) * 2)
            if after is not None:
                after(h, acc)

    def keep_edges(s):
        def after(h, acc):
            ye[s, 0, pl.ds(h * 8, 8), :] = acc[0]
            ye[s, 1, pl.ds(h * 8, 8), :] = acc[1]

        return after

    def start(l, r, j, h):
        writes, ends = [], []
        for c in range(CH):
            at = row_of(c, l, r), slice(None)
            q = 1.0 / diag_ref[cell(c, l, r)]
            value = cot_ref[cell(c, l, r)] + add_ref[at]
            g = cond_ref[cell(c, l, r)] * (value * q)
            writes.append((rhs, at, value))
            writes.append((inv, at, q))
            writes.append((g0, (pl.ds(grow_of(c, l, r), 8), slice(None)), g))
            ends.append(g)
        return writes, ends[0], ends[-1]

    def sums(g, s, l, r, j, h):
        own = [g[pl.ds(grow_of(c, l, r), 8), :] for c in range(CH)]
        before = pltpu.roll(yh[s, 0, pl.ds(h * 8, 8), :], 127 - j, 1)
        behind = pltpu.roll(yh[s, 1, pl.ds(h * 8, 8), :], (128 - j) % 128, 1)
        wide = [before, *own, behind]
        out = []
        for c in range(CH):
            b = grow_of(c, l, r)
            west = pltpu.roll(jnp.where(lane == 127, wide[c], own[c]), 1, 1)
            east = pltpu.roll(jnp.where(lane == 0, wide[c + 2], own[c]), 127, 1)
            total = g[pl.ds(b - 1, 8), :] + g[pl.ds(b + 1, 8), :]
            total = total + west + east
            out.append(total + g[pl.ds(b - SEG, 8), :] + g[pl.ds(b + SEG, 8), :])
        return out

    def first(l, r, j, h):
        writes, ends = [], []
        for c, total in enumerate(sums(g0, 0, l, r, j, h)):
            at = row_of(c, l, r), slice(None)
            g = cond_ref[cell(c, l, r)] * ((rhs[at] + total) * inv[at])
            writes.append((g1, (pl.ds(grow_of(c, l, r), 8), slice(None)), g))
            ends.append(g)
        return writes, ends[0], ends[-1]

    def second(l, r, j, h):
        writes = []
        for c, total in enumerate(sums(g1, 1, l, r, j, h)):
            at = row_of(c, l, r), slice(None)
            value = (rhs[at] + total) * inv[at]
            writes.append((adj, at, value))
            writes.append((out_ref, cell(c, l, r), value))
        return writes, None, None

    up, down = (tx + NX_DEV - 1) % NX_DEV, (tx + 1) % NX_DEV
    west, east = (ty + NY_DEV - 1) % NY_DEV, (ty + 1) % NY_DEV

    def halo(s, g):
        for c in range(CH):
            for l in range(NZ):
                n = c * NZ + l
                b = (c * (NZ + 2) + l + 1) * SEG + 8
                xe[s, 0, n : n + 1, :] = g[b : b + 1, :]
                xe[s, 1, n : n + 1, :] = g[b + CX - 1 : b + CX, :]
        if s == 0:
            pl.semaphore_wait(barrier, DEV - 1)
        copies = []
        for i, (src, dst, dev) in enumerate(
            (
                (ye.at[s, 0], yh.at[s, 1], (tx, west)),
                (ye.at[s, 1], yh.at[s, 0], (tx, east)),
                (xe.at[s, 0], xh.at[s, 1], (up, ty)),
                (xe.at[s, 1], xh.at[s, 0], (down, ty)),
            )
        ):
            copies.append(
                pltpu.make_async_remote_copy(
                    src_ref=src, dst_ref=dst, send_sem=hs.at[s, i], recv_sem=hr.at[s, i],
                    device_id=dev, device_id_type=MESH,
                )
            )
            copies[-1].start()
        for copy in copies:
            copy.wait()
        outer = jnp.where(tx == 0, 0.0, xh[s, 0])
        outer2 = jnp.where(tx == NX_DEV - 1, 0.0, xh[s, 1])
        for c in range(CH):
            for l in range(NZ):
                n = c * NZ + l
                b = (c * (NZ + 2) + l + 1) * SEG + 8
                g[b - 1 : b, :] = outer[n : n + 1, :]
                g[b + CX : b + CX + 1, :] = outer2[n : n + 1, :]
        yh[s, 0] = jnp.where(ty == 0, 0.0, yh[s, 0])
        yh[s, 1] = jnp.where(ty == NY_DEV - 1, 0.0, yh[s, 1])

    visit(start, keep_edges(0))
    halo(0, g0)
    visit(first, keep_edges(1))
    halo(1, g1)
    visit(second)

    def take(q):
        for u in range(CAP):
            heat[pl.ds(u, 1), :] = adj[pl.ds(idx_s[q, u], 1), :]
        hsend[q] = heat[...].astype(BF16)

    def post(g, i):
        a, b = to(g, i)
        q = b * NX_DEV + a
        take(q)
        pltpu.make_async_remote_copy(
            src_ref=hsend.at[q], dst_ref=recv.at[me_t], send_sem=ssem,
            recv_sem=rsem, device_id=(a, b), device_id_type=MESH,
        ).start()

    each(post)
    take(me_q)
    own = pltpu.make_async_copy(hsend.at[me_q], recv.at[me_t], lsem)
    own.start()

    own.wait()

    wait_for(hsend, recv, DEV - 1, 0, ssem, rsem, to(0, 1)).wait()

    @pl.loop(0, DEV // 4)
    def _(i):
        recvf[pl.ds(pl.multiple_of(i * 128, 128), 128), :] = (
            recv[pl.ds(i * 4, 4)].reshape(128, 128).astype(F32)
        )


def pull_kernel(slot_s, recvf, kb_ref, spread_ref, deriv_ref, temp_ref, out_ref, grad_ref, even, odd, sem):
    save = pltpu.make_async_copy(temp_ref, out_ref, sem)
    save.start()

    def gather(i, rows):
        for n in range(256):
            rows[n : n + 1, :] = recvf[pl.ds(slot_s[i * 2 + n // 128, n % 128], 1), :]

    def pull(i, rows):
        at = pl.ds(pl.multiple_of(i * 256, 256), 256)
        x = rows[...].astype(BF16)
        kb = kb_ref[at, :]
        zero = jnp.zeros_like(x)
        masked = jnp.concatenate(
            [jnp.where(kb == jnp.asarray(k, BF16), x, zero) for k in range(KINDS)], axis=1
        )
        wide = jnp.concatenate([spread_ref[k] for k in range(KINDS)], axis=1)
        total = lax.dot_general(masked, wide, NT, preferred_element_type=F32)
        grad_ref[at, :] = deriv_ref[at, :] * total

    gather(0, even)

    @pl.loop(0, 4)
    def _(i):
        gather(2 * i + 1, odd)
        pull(2 * i, even)
        gather(jnp.minimum(2 * i + 2, 7), even)
        pull(2 * i + 1, odd)

    save.wait()


def local(cot_field, conductance, diagonal, source_adjoint, spreading, heat_deriv, block_tile, block_patch, block_kind):
    grid16 = (OWNED // 128, 128)
    shape = jax.ShapeDtypeStruct
    dma = pltpu.SemaphoreType.DMA
    seeds, idx, got, slots, kinds = pl.pallas_call(
        forward_kernel,
        out_shape=(
            shape((SLOTS, 128), F32),
            shape((DEV, 128), I32),
            shape((DEV, 128), I32),
            shape(grid16, I32),
            shape((OWNED, 128), BF16),
        ),
        in_specs=[VMEM] * 3,
        out_specs=(VMEM,) * 5,
        scratch_shapes=[
            pltpu.VMEM((OWNED, 128), F32),
            pltpu.VMEM((CAP, 128), F32),
            pltpu.VMEM((DEV, CAP, 128), BF16),
            pltpu.VMEM((NX_DEV, NY_DEV, 128), I32),
            pltpu.VMEM((CAP, DEV), I32),
            pltpu.SMEM((CAP, DEV), I32),
            pltpu.VMEM((DEV, CAP, 128), BF16),
            pltpu.VMEM((NX_DEV, NY_DEV, 128), I32),
            pltpu.VMEM((NY_DEV, NX_DEV, 128), I32),
            pltpu.VMEM((NY_DEV, NX_DEV, 128), I32),
            pltpu.VMEM((CAP, DEV), F32),
            dma,
            dma((NY_DEV,)),
            dma((NX_DEV,)),
            dma((NX_DEV,)),
            dma((NY_DEV,)),
            dma((NY_DEV,)),
            dma((4,)),
        ],
        compiler_params=pltpu.CompilerParams(
            collective_id=0, has_side_effects=True, vmem_limit_bytes=12 << 20
        ),
        name="forward",
    )(
        jnp.concatenate([x.reshape(grid16) for x in (block_tile, block_patch, block_kind)]),
        source_adjoint,
        spreading.reshape(KINDS * 128, 128),
    )

    hbm = pl.BlockSpec(memory_space=pltpu.MemorySpace.HBM)
    added, *fields = pl.pallas_call(
        scatter_kernel,
        out_shape=(shape((ROWS, 128), F32),) + (shape(cot_field.shape, F32),) * 3,
        in_specs=[SMEM, SMEM, VMEM] + [hbm] * 3,
        out_specs=(VMEM,) * 4,
        scratch_shapes=[dma((3,))],
        compiler_params=pltpu.CompilerParams(vmem_limit_bytes=36 << 20),
        name="scatter",
    )(idx, got, seeds, cot_field, conductance, diagonal)

    flat = pltpu.VMEM((PATCHES, 128), F32)
    padded = pltpu.VMEM((GROWS, 128), F32)
    temp, heat = pl.pallas_call(
        backward_kernel,
        out_shape=(shape(cot_field.shape, F32), shape((SLOTS, 128), F32)),
        in_specs=[SMEM] + [VMEM] * 4,
        out_specs=(VMEM, VMEM),
        scratch_shapes=[
            flat,
            flat,
            padded,
            padded,
            pltpu.VMEM((ROWS, 128), F32),
            pltpu.VMEM((CAP, 128), F32),
            pltpu.VMEM((DEV, CAP, 128), BF16),
            pltpu.VMEM((DEV, CAP, 128), BF16),
            pltpu.VMEM((2, 2, CH * NZ, 128), F32),
            pltpu.VMEM((2, 2, 16, 128), F32),
            pltpu.VMEM((2, 2, CH * NZ, 128), F32),
            pltpu.VMEM((2, 2, 16, 128), F32),
            dma,
            dma,
            dma((2, 4)),
            dma((2, 4)),
            dma,
        ],
        compiler_params=pltpu.CompilerParams(
            collective_id=1, has_side_effects=True, vmem_limit_bytes=30 << 20
        ),
        name="backward",
    )(idx, *fields, added)

    return pl.pallas_call(
        pull_kernel,
        out_shape=(shape(cot_field.shape, F32), shape((OWNED, 128), F32)),
        in_specs=[SMEM, VMEM, VMEM, VMEM, VMEM, VMEM],
        out_specs=(ANY, VMEM),
        scratch_shapes=[pltpu.VMEM((256, 128), F32), pltpu.VMEM((256, 128), F32), dma],
        compiler_params=pltpu.CompilerParams(vmem_limit_bytes=16 << 20),
        name="pull",
    )(slots, heat, kinds, spreading, heat_deriv, temp)


def solution(mesh):
    blocks = P(("tx", "ty"))
    field = P(None, "tx", "ty")
    in_specs = (
        field, field, field, P(("tx", "ty"), None), P(), P(("tx", "ty"), None),
        P(("tx", "ty"), None), blocks, blocks,
    )
    out_specs = (field, P(("tx", "ty"), None))
    return jax.shard_map(local, mesh=mesh, in_specs=in_specs, out_specs=out_specs, check_vma=False)
```

```python
import functools

import jax
import jax.numpy as jnp
from jax import lax
from jax.experimental import pallas as pl
from jax.experimental.pallas import tpu as pltpu
from jax.sharding import PartitionSpec as P

NX_DEV, NY_DEV = 8, 16
DEV = NX_DEV * NY_DEV
CAP = 32
SLOTS = DEV * CAP
KINDS = 16
NZ, CX, CY = 8, 256, 512
CH = CY // 128
PATCHES = NZ * CX * CH
ROWS = PATCHES + CAP
SEG = CX + 16
GROWS = CH * (NZ + 2) * SEG
OWNED = 2048
GROUP = 8
CLASH = 8
AHEAD = 6
UNROLL, BATCH = 16, 1
F32, BF16, I32 = jnp.float32, jnp.bfloat16, jnp.int32
MESH = pl.DeviceIdType.MESH
VMEM = pl.BlockSpec(memory_space=pltpu.VMEM)
SMEM = pl.BlockSpec(memory_space=pltpu.SMEM)
ANY = pl.BlockSpec(memory_space=pl.ANY)
NT = (((1,), (1,)), ((), ()))


def dot(a, b):
    return jnp.dot(a, b, preferred_element_type=F32)


def iota(shape, dim):
    return lax.broadcasted_iota(I32, shape, dim)


def route(table_ref, slot_ref, kb_ref):
    sub, lane = iota((128, 128), 0), iota((128, 128), 1)
    before = (sub < lane).astype(F32).astype(BF16)
    ones = jnp.ones((128, 128), BF16)
    rank_row = iota((CAP, 128), 0)
    count = jnp.zeros((128, 128), F32)
    held = jnp.zeros((128, 128), F32)
    block = jnp.zeros((CAP, 128), F32)
    for j in range(OWNED // 128):
        tile, patch, kind = (table_ref[n * 16 + j : n * 16 + j + 1, :] for n in range(3))
        place = (patch & (CH - 1)) * (NZ * CX) + (patch >> 2)
        hit = (sub == tile).astype(F32)
        hit16 = hit.astype(BF16)
        rank = jnp.sum(hit * (dot(hit16, before) + count), axis=0, keepdims=True).astype(I32)
        count = count + dot(hit16, ones)
        slot_ref[j : j + 1, :] = tile * CAP + rank
        at = (rank_row == rank).astype(F32)
        parts = jnp.concatenate(
            [
                at * (place >> 7).astype(F32),
                at * (place & 127).astype(F32),
                at * (kind + 1).astype(F32),
                jnp.zeros((128 - 3 * CAP, 128), F32),
            ],
            axis=0,
        ).astype(BF16)
        held = held + lax.dot_general(hit16, parts, NT, preferred_element_type=F32)
        numbers = jnp.concatenate([at * iota((1, 128), 1).astype(F32), at], axis=0).astype(BF16)
        found = lax.dot_general(numbers, hit16, NT, preferred_element_type=F32)
        block = block + found[:CAP] + found[CAP:] * (128.0 * j)
        kb_ref[pl.ds(j * 128, 128), :] = jnp.transpose(
            jnp.broadcast_to(kind.astype(F32), (128, 128))
        ).astype(BF16)
    counts = count.astype(I32)
    place = (held * 128.0 + pltpu.roll(held, 128 - CAP, 1)).astype(I32)
    kind1 = pltpu.roll(held, 128 - 2 * CAP, 1).astype(I32)
    place = jnp.where(lane < counts, place, PATCHES + lane)
    clash = jnp.zeros((128, 128), I32)
    for k in range(1, CAP):
        same = (pltpu.roll(place, k, 1) == place) & (lane >= k) & (lane < counts)
        clash = jnp.maximum(clash, same.astype(I32))
    clash = jnp.max(clash, axis=1, keepdims=True)
    groups = (counts + (GROUP - 1)) // GROUP + clash * CLASH
    return jnp.where(lane < CAP, place + kind1 * 16384, groups), block.astype(I32) & (OWNED - 1)


def partners():
    tx, ty = lax.axis_index("tx"), lax.axis_index("ty")

    def to(g, i):
        return lax.rem(tx + i, NX_DEV), lax.rem(ty + g * 5, NY_DEV)

    def from_y(g):
        return lax.rem(ty + 5 * NY_DEV - g * 5, NY_DEV)

    return tx, ty, to, from_y


def each(*steps, lo=0, hi=NY_DEV):
    if lo == 0:
        for step in steps:
            for i in range(1, NX_DEV):
                step(0, i)

    @pl.loop(max(lo, 1), hi)
    def _(g):
        for step in steps:
            for i in range(NX_DEV):
                step(g, i)


def greet_all(to):
    barrier = pltpu.get_barrier_semaphore()
    each(
        lambda g, i: pl.semaphore_signal(barrier, inc=1, device_id=to(g, i), device_id_type=MESH)
    )
    return barrier


def wait_for(src, dst, n, at, send_sem, recv_sem, peer):
    return pltpu.make_async_remote_copy(
        src_ref=src.at[pl.ds(at, n)], dst_ref=dst.at[pl.ds(at, n)],
        send_sem=send_sem, recv_sem=recv_sem, device_id=peer, device_id_type=MESH,
    )


def forward_kernel(
    table_ref, src_ref, spread_ref,
    seed_ref, idx_ref, meta_ref, slot_ref, kb_ref,
    srcf, rows_f, send, mine, block_v, block_s, recv, mid, mid2, last, kcol,
    ssem, rsem, xs, xr, ys, yr, lsem,
):
    tx, ty, to, from_y = partners()
    me_t, me_q = tx * NY_DEV + ty, ty * NX_DEV + tx
    barrier = greet_all(to)
    meta, block = route(table_ref, slot_ref, kb_ref)
    block_v[...] = block
    fetch = pltpu.make_async_copy(block_v, block_s, lsem.at[3])
    fetch.start()
    for i in range(NX_DEV):
        mine[i] = meta[i * NY_DEV : (i + 1) * NY_DEV, :]
    own_mid = pltpu.make_async_copy(mine.at[tx], mid.at[tx], lsem.at[1])
    own_mid.start()

    @pl.loop(0, OWNED // 128)
    def _(i):
        at = pl.ds(pl.multiple_of(i * 128, 128), 128)
        srcf[at, :] = src_ref[at, :].astype(F32)

    fetch.wait()
    pl.semaphore_wait(barrier, DEV - 1)

    def pack(t, i):
        for u in range(CAP):
            rows_f[i, u : u + 1, :] = srcf[pl.ds(block_s[u, t], 1), :]
        send[t] = rows_f[i].astype(BF16)

    def x_copy(i, peer, there):
        return pltpu.make_async_remote_copy(
            src_ref=mine.at[peer], dst_ref=mid.at[there], send_sem=xs.at[i],
            recv_sem=xr.at[i], device_id=(peer, ty), device_id_type=MESH,
        )

    def y_copy(i, peer, there):
        return pltpu.make_async_remote_copy(
            src_ref=mid2.at[peer], dst_ref=last.at[there], send_sem=ys.at[i],
            recv_sem=yr.at[i], device_id=(tx, peer), device_id_type=MESH,
        )


    @pl.loop(1, NX_DEV)
    def _(i):
        x_copy(i, (tx + i) % NX_DEV, tx).start()

    def send_one(g, i):
        a, b = to(g, i)
        t = a * NY_DEV + b
        pack(t, i)
        pltpu.make_async_remote_copy(
            src_ref=send.at[t], dst_ref=recv.at[me_q], send_sem=ssem,
            recv_sem=rsem.at[g], device_id=(a, b), device_id_type=MESH,
        ).start()

    each(send_one, lo=0, hi=2)
    own_mid.wait()

    @pl.loop(1, NX_DEV)
    def _(i):
        x_copy(i, (tx + NX_DEV - i) % NX_DEV, (tx + NX_DEV - i) % NX_DEV).wait()

    for j in range(NY_DEV):
        mid2[j] = mid[:, j, :]
    own_meta = pltpu.make_async_copy(mid2.at[ty], last.at[ty], lsem.at[2])
    own_meta.start()

    @pl.loop(1, NY_DEV)
    def _(i):
        y_copy(i, (ty + i) % NY_DEV, ty).start()

    each(send_one, lo=2, hi=AHEAD)
    pack(me_t, 0)
    own = pltpu.make_async_copy(send.at[me_t], recv.at[me_q], lsem.at[0])
    own.start()
    own_meta.wait()
    own.wait()

    @pl.loop(1, NY_DEV)
    def _(i):
        y_copy(i, (ty + NY_DEV - i) % NY_DEV, (ty + NY_DEV - i) % NY_DEV).wait()

    meta = last[...].reshape(DEV, 128)
    meta_ref[...] = meta
    idx_ref[...] = meta & 16383
    kind1 = jnp.transpose(((meta >> 14) & 31).astype(F32))[:CAP, :]
    kcol[...] = kind1

    @pl.loop(0, NY_DEV)
    def _(g):
        @pl.when(g < NY_DEV - AHEAD)
        def _():
            for i in range(NX_DEV):
                send_one(g + AHEAD, i)

        q = from_y(g)

        @pl.when(g == 0)
        def _():
            wait_for(send, recv, NX_DEV - 1, 0, ssem, rsem.at[0], to(0, 1)).wait_recv()

        @pl.when(g > 0)
        def _():
            wait_for(send, recv, NX_DEV, q * NX_DEV, ssem, rsem.at[g], to(0, 1)).wait_recv()

        kinds = pltpu.roll(kcol[...], (DEV - q * NX_DEV) % DEV, 1)
        kb = jnp.concatenate(
            [jnp.broadcast_to(kinds[:, i : i + 1], (CAP, 128)) for i in range(NX_DEV)], axis=0
        ).astype(BF16)
        x = recv[pl.ds(q * NX_DEV, NX_DEV)].reshape(NX_DEV * CAP, 128)
        zero = jnp.zeros_like(x)
        masked = jnp.concatenate(
            [jnp.where(kb == jnp.asarray(k + 1, BF16), x, zero) for k in range(KINDS)], axis=1
        )
        rows = pl.ds(pl.multiple_of(q * (NX_DEV * CAP), NX_DEV * CAP), NX_DEV * CAP)
        seed_ref[rows, :] = dot(masked, spread_ref[...])

    wait_for(send, recv, DEV - 1, 0, ssem, rsem.at[0], to(0, 1)).wait_send()


def scatter_kernel(idx_s, meta_s, seed_ref, *refs):
    fields, acc, held, sem = refs[:3], refs[3], refs[4:7], refs[7]
    loads = [pltpu.make_async_copy(f, h, sem.at[n]) for n, (f, h) in enumerate(zip(fields, held))]
    for load in loads:
        load.start()

    @pl.loop(0, ROWS // 32)
    def _(i):
        acc[pl.ds(pl.multiple_of(i * 32, 32), 32), :] = jnp.zeros((32, 128), F32)

    @pl.loop(0, DEV)
    def _(q):
        groups = meta_s[q, CAP]
        base = pl.multiple_of(q * CAP, CAP)
        for n in range(1, CAP // GROUP + 1):

            @pl.when(groups == n)
            def _():
                at = [pl.ds(idx_s[q, u], 1) for u in range(n * GROUP)]
                new = [acc[at[u], :] + seed_ref[pl.ds(base + u, 1), :] for u in range(n * GROUP)]
                for u in range(n * GROUP):
                    acc[at[u], :] = new[u]

        @pl.when(groups > CLASH)
        def _():
            for u in range(CAP):
                at = pl.ds(idx_s[q, u], 1)
                acc[at, :] = acc[at, :] + seed_ref[pl.ds(base + u, 1), :]

    for load in loads:
        load.wait()


def backward_kernel(
    idx_s, cot_ref, cond_ref, diag_ref, add_ref,
    out_ref, recvf,
    rhs, inv, g0, g1, adj, heat, hsend, recv,
    xe, ye, xh, yh,
    ssem, rsem, hs, hr, lsem,
):
    tx, ty, to, from_y = partners()
    me_t, me_q = tx * NY_DEV + ty, ty * NX_DEV + tx
    fetch = pltpu.make_async_copy(add_ref, adj, lsem)
    fetch.start()
    lane = iota((8, 128), 1)
    barrier = greet_all(to)
    for g in (g0, g1):
        for c in range(CH):
            for l in (0, NZ + 1):

                @pl.loop(0, CX // 64)
                def _(i):
                    g[pl.ds((c * (NZ + 2) + l) * SEG + 8 + i * 64, 64), :] = jnp.zeros((64, 128), F32)

    def cell(c, l, r):
        return l, pl.ds(r, 8), pl.ds(c * 128, 128)

    def row_of(c, l, r):
        return pl.ds(pl.multiple_of(c * (NZ * CX) + l * CX + r, 8), 8)

    def grow_of(c, l, r):
        return pl.multiple_of((c * (NZ + 2) + l + 1) * SEG + 8 + r, 8)

    def edges(acc, lo, hi, j):
        left, right = acc
        left = jnp.where(lane == j, pltpu.roll(lo, j, 1), left)
        right = jnp.where(lane == j, pltpu.roll(hi, (j + 1) % 128, 1), right)
        return left, right

    def visit(body, after=None):
        for h in range(2):

            def step(i, acc):
                for v in range(0, UNROLL, BATCH):
                    stores = []
                    for u in range(v, v + BATCH):
                        j = i * UNROLL + u
                        r = pl.multiple_of((i % (32 // UNROLL)) * (UNROLL * 8), 8) + u * 8
                        writes, lo, hi = body(h * 4 + i // (32 // UNROLL), r, j, h)
                        stores += writes
                        if after is not None:
                            acc = edges(acc, lo, hi, j)
                    for ref, at, value in stores:
                        ref[at] = value
                return acc

            acc = lax.fori_loop(0, 128 // UNROLL, step, (jnp.zeros((8, 128), F32),) * 2)
            if after is not None:
                after(h, acc)

    def keep_edges(s):
        def after(h, acc):
            ye[s, 0, pl.ds(h * 8, 8), :] = acc[0]
            ye[s, 1, pl.ds(h * 8, 8), :] = acc[1]

        return after

    def start(l, r, j, h):
        writes, ends = [], []
        for c in range(CH):
            at = row_of(c, l, r), slice(None)
            q = 1.0 / diag_ref[cell(c, l, r)]
            value = cot_ref[cell(c, l, r)] + adj[at]
            g = cond_ref[cell(c, l, r)] * (value * q)
            writes.append((rhs, at, value))
            writes.append((inv, at, q))
            writes.append((g0, (pl.ds(grow_of(c, l, r), 8), slice(None)), g))
            ends.append(g)
        return writes, ends[0], ends[-1]

    def sums(g, s, l, r, j, h):
        own = [g[pl.ds(grow_of(c, l, r), 8), :] for c in range(CH)]
        before = pltpu.roll(yh[s, 0, pl.ds(h * 8, 8), :], 127 - j, 1)
        behind = pltpu.roll(yh[s, 1, pl.ds(h * 8, 8), :], (128 - j) % 128, 1)
        wide = [before, *own, behind]
        out = []
        for c in range(CH):
            b = grow_of(c, l, r)
            west = pltpu.roll(jnp.where(lane == 127, wide[c], own[c]), 1, 1)
            east = pltpu.roll(jnp.where(lane == 0, wide[c + 2], own[c]), 127, 1)
            total = g[pl.ds(b - 1, 8), :] + g[pl.ds(b + 1, 8), :]
            total = total + west + east
            out.append(total + g[pl.ds(b - SEG, 8), :] + g[pl.ds(b + SEG, 8), :])
        return out

    def first(l, r, j, h):
        writes, ends = [], []
        for c, total in enumerate(sums(g0, 0, l, r, j, h)):
            at = row_of(c, l, r), slice(None)
            g = cond_ref[cell(c, l, r)] * ((rhs[at] + total) * inv[at])
            writes.append((g1, (pl.ds(grow_of(c, l, r), 8), slice(None)), g))
            ends.append(g)
        return writes, ends[0], ends[-1]

    def second(l, r, j, h):
        writes = []
        for c, total in enumerate(sums(g1, 1, l, r, j, h)):
            at = row_of(c, l, r), slice(None)
            value = (rhs[at] + total) * inv[at]
            writes.append((adj, at, value))
            writes.append((out_ref, cell(c, l, r), value))
        return writes, None, None

    up, down = (tx + NX_DEV - 1) % NX_DEV, (tx + 1) % NX_DEV
    west, east = (ty + NY_DEV - 1) % NY_DEV, (ty + 1) % NY_DEV

    def halo(s, g):
        for c in range(CH):
            for l in range(NZ):
                n = c * NZ + l
                b = (c * (NZ + 2) + l + 1) * SEG + 8
                xe[s, 0, n : n + 1, :] = g[b : b + 1, :]
                xe[s, 1, n : n + 1, :] = g[b + CX - 1 : b + CX, :]
        if s == 0:
            pl.semaphore_wait(barrier, DEV - 1)
        copies = []
        for i, (src, dst, dev) in enumerate(
            (
                (ye.at[s, 0], yh.at[s, 1], (tx, west)),
                (ye.at[s, 1], yh.at[s, 0], (tx, east)),
                (xe.at[s, 0], xh.at[s, 1], (up, ty)),
                (xe.at[s, 1], xh.at[s, 0], (down, ty)),
            )
        ):
            copies.append(
                pltpu.make_async_remote_copy(
                    src_ref=src, dst_ref=dst, send_sem=hs.at[s, i], recv_sem=hr.at[s, i],
                    device_id=dev, device_id_type=MESH,
                )
            )
            copies[-1].start()
        for copy in copies:
            copy.wait()
        outer = jnp.where(tx == 0, 0.0, xh[s, 0])
        outer2 = jnp.where(tx == NX_DEV - 1, 0.0, xh[s, 1])
        for c in range(CH):
            for l in range(NZ):
                n = c * NZ + l
                b = (c * (NZ + 2) + l + 1) * SEG + 8
                g[b - 1 : b, :] = outer[n : n + 1, :]
                g[b + CX : b + CX + 1, :] = outer2[n : n + 1, :]
        yh[s, 0] = jnp.where(ty == 0, 0.0, yh[s, 0])
        yh[s, 1] = jnp.where(ty == NY_DEV - 1, 0.0, yh[s, 1])

    fetch.wait()
    visit(start, keep_edges(0))
    halo(0, g0)
    visit(first, keep_edges(1))
    halo(1, g1)
    visit(second)

    def take(q, i):
        for u in range(CAP):
            heat[i, u : u + 1, :] = adj[pl.ds(idx_s[q, u], 1), :]
        hsend[q] = heat[i].astype(BF16)

    def ready(g, i):
        a, b = to(g, i)
        take(b * NX_DEV + a, i)

    def post(g, i):
        a, b = to(g, i)
        pltpu.make_async_remote_copy(
            src_ref=hsend.at[b * NX_DEV + a], dst_ref=recv.at[me_t], send_sem=ssem,
            recv_sem=rsem, device_id=(a, b), device_id_type=MESH,
        ).start()

    each(ready, post)
    take(me_q, 0)
    own = pltpu.make_async_copy(hsend.at[me_q], recv.at[me_t], lsem)
    own.start()

    own.wait()

    wait_for(hsend, recv, DEV - 1, 0, ssem, rsem, to(0, 1)).wait()

    @pl.loop(0, DEV // 4)
    def _(i):
        recvf[pl.ds(pl.multiple_of(i * 128, 128), 128), :] = (
            recv[pl.ds(i * 4, 4)].reshape(128, 128).astype(F32)
        )


def pull_kernel(slot_s, recvf, kb_ref, spread_ref, deriv_ref, temp_ref, out_ref, grad_ref, even, odd, sem):
    save = pltpu.make_async_copy(temp_ref, out_ref, sem)
    save.start()

    def gather(i, rows):
        for n in range(256):
            rows[n : n + 1, :] = recvf[pl.ds(slot_s[i * 2 + n // 128, n % 128], 1), :]

    def pull(i, rows):
        at = pl.ds(pl.multiple_of(i * 256, 256), 256)
        x = rows[...].astype(BF16)
        kb = kb_ref[at, :]
        zero = jnp.zeros_like(x)
        masked = jnp.concatenate(
            [jnp.where(kb == jnp.asarray(k, BF16), x, zero) for k in range(KINDS)], axis=1
        )
        wide = jnp.concatenate([spread_ref[k] for k in range(KINDS)], axis=1)
        total = lax.dot_general(masked, wide, NT, preferred_element_type=F32)
        grad_ref[at, :] = deriv_ref[at, :] * total

    gather(0, even)

    @pl.loop(0, 4)
    def _(i):
        gather(2 * i + 1, odd)
        pull(2 * i, even)
        gather(jnp.minimum(2 * i + 2, 7), even)
        pull(2 * i + 1, odd)

    save.wait()


def local(cot_field, conductance, diagonal, source_adjoint, spreading, heat_deriv, block_tile, block_patch, block_kind):
    grid16 = (OWNED // 128, 128)
    shape = jax.ShapeDtypeStruct
    dma = pltpu.SemaphoreType.DMA
    seeds, idx, got, slots, kinds = pl.pallas_call(
        forward_kernel,
        out_shape=(
            shape((SLOTS, 128), F32),
            shape((DEV, 128), I32),
            shape((DEV, 128), I32),
            shape(grid16, I32),
            shape((OWNED, 128), BF16),
        ),
        in_specs=[VMEM] * 3,
        out_specs=(VMEM,) * 5,
        scratch_shapes=[
            pltpu.VMEM((OWNED, 128), F32),
            pltpu.VMEM((NX_DEV, CAP, 128), F32),
            pltpu.VMEM((DEV, CAP, 128), BF16),
            pltpu.VMEM((NX_DEV, NY_DEV, 128), I32),
            pltpu.VMEM((CAP, DEV), I32),
            pltpu.SMEM((CAP, DEV), I32),
            pltpu.VMEM((DEV, CAP, 128), BF16),
            pltpu.VMEM((NX_DEV, NY_DEV, 128), I32),
            pltpu.VMEM((NY_DEV, NX_DEV, 128), I32),
            pltpu.VMEM((NY_DEV, NX_DEV, 128), I32),
            pltpu.VMEM((CAP, DEV), F32),
            dma,
            dma((NY_DEV,)),
            dma((NX_DEV,)),
            dma((NX_DEV,)),
            dma((NY_DEV,)),
            dma((NY_DEV,)),
            dma((4,)),
        ],
        compiler_params=pltpu.CompilerParams(
            collective_id=0, has_side_effects=True, vmem_limit_bytes=12 << 20
        ),
        name="forward",
    )(
        jnp.concatenate([x.reshape(grid16) for x in (block_tile, block_patch, block_kind)]),
        source_adjoint,
        spreading.reshape(KINDS * 128, 128),
    )

    hbm = pl.BlockSpec(memory_space=pltpu.MemorySpace.HBM)
    added, *fields = pl.pallas_call(
        scatter_kernel,
        out_shape=(shape((ROWS, 128), F32),) + (shape(cot_field.shape, F32),) * 3,
        in_specs=[SMEM, SMEM, VMEM] + [hbm] * 3,
        out_specs=(VMEM,) * 4,
        scratch_shapes=[dma((3,))],
        compiler_params=pltpu.CompilerParams(vmem_limit_bytes=36 << 20),
        name="scatter",
    )(idx, got, seeds, cot_field, conductance, diagonal)

    flat = pltpu.VMEM((PATCHES, 128), F32)
    padded = pltpu.VMEM((GROWS, 128), F32)
    temp, heat = pl.pallas_call(
        backward_kernel,
        out_shape=(shape(cot_field.shape, F32), shape((SLOTS, 128), F32)),
        in_specs=[SMEM] + [VMEM] * 3 + [ANY],
        out_specs=(VMEM, VMEM),
        scratch_shapes=[
            flat,
            flat,
            padded,
            padded,
            pltpu.VMEM((ROWS, 128), F32),
            pltpu.VMEM((NX_DEV, CAP, 128), F32),
            pltpu.VMEM((DEV, CAP, 128), BF16),
            pltpu.VMEM((DEV, CAP, 128), BF16),
            pltpu.VMEM((2, 2, CH * NZ, 128), F32),
            pltpu.VMEM((2, 2, 16, 128), F32),
            pltpu.VMEM((2, 2, CH * NZ, 128), F32),
            pltpu.VMEM((2, 2, 16, 128), F32),
            dma,
            dma,
            dma((2, 4)),
            dma((2, 4)),
            dma,
        ],
        compiler_params=pltpu.CompilerParams(
            collective_id=1, has_side_effects=True, vmem_limit_bytes=33 << 20
        ),
        name="backward",
    )(idx, *fields, added)

    return pl.pallas_call(
        pull_kernel,
        out_shape=(shape(cot_field.shape, F32), shape((OWNED, 128), F32)),
        in_specs=[SMEM, VMEM, VMEM, VMEM, VMEM, VMEM],
        out_specs=(ANY, VMEM),
        scratch_shapes=[pltpu.VMEM((256, 128), F32), pltpu.VMEM((256, 128), F32), dma],
        compiler_params=pltpu.CompilerParams(vmem_limit_bytes=16 << 20),
        name="pull",
    )(slots, heat, kinds, spreading, heat_deriv, temp)


def solution(mesh):
    blocks = P(("tx", "ty"))
    field = P(None, "tx", "ty")
    in_specs = (
        field, field, field, P(("tx", "ty"), None), P(), P(("tx", "ty"), None),
        P(("tx", "ty"), None), blocks, blocks,
    )
    out_specs = (field, P(("tx", "ty"), None))
    return jax.shard_map(local, mesh=mesh, in_specs=in_specs, out_specs=out_specs, check_vma=False)
```
